256 devices in a mesh: seq: 8 (over x, core), tensor: 32 (over y, z).
Axes of the slice: x: 4, y: 4, z: 8, core: 2. Of those that a mesh axis runs over, the one named last changes fastest.
Arguments:
- token_ids: int32 [2, 7], replicated, may hold values from 0 to 131071
- cache_lengths: int32 [7], replicated, may hold values from 1 to 10238
- embed_table: bfloat16 [131072, 4096], P('seq', 'tensor'), may hold values from -64 to 64
- attn_gain: float32 [4096], replicated, may hold values from 0.1 to 1.9
- final_gain: float32 [4096], replicated, may hold values from 0.1 to 1.9
- w_qkv: bfloat16 [4096, 3, 4096], P(None, None, 'tensor'), may hold values from -0.09375 to 0.09375
- w_out: bfloat16 [4096, 4096], P('tensor'), may hold values from -0.09375 to 0.09375
- cache_keys: bfloat16 [7, 10240, 4096], P(None, 'seq', 'tensor'), may hold values from -300 to 300
- cache_values: bfloat16 [7, 10240, 4096], P(None, 'seq', 'tensor'), may hold values from -24 to 24
Outputs:
- hidden: bfloat16 [2, 7, 4096], P(None, None, 'tensor')
- new_kv: bfloat16 [2, 2, 7, 4096], P(None, None, None, 'tensor')
- logprobs: float32 [2, 7, 131072], P(None, None, ('seq', 'tensor'))
The draws below stay inside these ranges and needn't reach their ends.
All inputs are finite; a program needn't handle non-finite values.
Results may differ from the reference program's by a relative error of at most 0.0085.
The reference program's roundings to bfloat16 on the way (of `embedded`, `normed`, `queries`, `attended` and `gated_rows`) count: a program that leaves them out, or rounds other values in their place, can miss the bound.
Values may be sent and summed in bfloat16 or wider, within the bound.
No kernel may reach another device: no remote copies, remote signals or barrier semaphores. Data moves between devices by JAX's collectives and lax.ppermute only.
A program may use at most 64 MiB of HBM per device.

```python
import math
import jax
import jax.numpy as jnp
from jax import lax

HD = 128
D = 4096
V = 131072
STREAMS = 7
CTX = 10240


def draw_embed_table(key, part):
    base_key = jax.random.fold_in(jax.random.fold_in(key, 11), 0)
    table = 0.25 * jnp.clip(jax.random.normal(base_key, (V, D), jnp.float32), -4.0, 4.0)
    position = jnp.arange(D, dtype=jnp.float32) / (D - 1)
    vocab_position = jnp.arange(V, dtype=jnp.float32) / (V - 1)
    row_rise = jnp.exp(vocab_position * math.log(3.0))[:, None]
    column_scale = jnp.exp(position * math.log(4.0))
    row_scale = row_rise
    table = table * row_scale * column_scale[None, :]
    return table.astype(jnp.bfloat16)


def draw_cache_keys(key, part):
    base_key = jax.random.fold_in(jax.random.fold_in(key, 23), 0)
    keys_drawn = jnp.clip(jax.random.normal(base_key, (STREAMS, CTX, D), jnp.float32), -5.0, 5.0)
    return keys_drawn.astype(jnp.bfloat16)


def with_ends(entries, stream_key, low, largest):
    extent = entries.shape
    index_at = [jax.random.randint(jax.random.fold_in(stream_key, axis), (), 0, extent[axis]) for axis in range(len(extent))]
    entries = entries.at[tuple(index_at)].set(low)
    longest = extent.index(max(extent))
    index_at[longest] = (index_at[longest] + 1) % extent[longest]
    return entries.at[tuple(index_at)].set(largest)


def shard_levels(rng, dims, shards, low, high):
    gain, own = 1.0, jax.random.fold_in(rng, 6)
    for axis_at, parts in shards:
        heights = jnp.exp(jax.random.uniform(jax.random.fold_in(own, axis_at), (parts,), jnp.float32, low / len(shards), high / len(shards)))
        gain = gain * jnp.repeat(heights, dims[axis_at] // parts).reshape([-1 if axis == axis_at else 1 for axis in range(len(dims))])
    return gain


def noise(own_key, extent, width, most, cuts=(), kind=jnp.bfloat16):
    entries = jax.random.normal(own_key, extent, jnp.float32) * width
    if len(cuts) > 0:
        entries = shard_levels(own_key, extent, cuts, -0.22, 0.18) * entries
    return jnp.clip(entries, min=-most, max=most).astype(kind)


def setup_inputs(seed: int = 0) -> dict:
    keys = jax.random.split(jax.random.key(seed), 10)
    return {
        "token_ids": with_ends(jax.random.randint(keys[0], (2, STREAMS), 0, V), jax.random.fold_in(keys[0], 1), 0, V - 1).astype(jnp.int32),
        "cache_lengths": with_ends(jax.random.randint(keys[1], (STREAMS,), 1, CTX - 1), jax.random.fold_in(keys[1], 1), 1, (CTX - 1) - 1).astype(jnp.int32),
        "embed_table": draw_embed_table(jax.random.fold_in(keys[9], 71), 0),
        "attn_gain": jnp.clip(1.0 + 0.18 * jax.random.normal(keys[3], (D,), jnp.float32), 0.1, 1.9),
        "final_gain": jnp.clip(1.0 + 0.18 * jax.random.normal(keys[4], (D,), jnp.float32), 0.1, 1.9),
        "w_qkv": noise(keys[5], (D, 3, D), D ** -0.5, 0.09375, ((2, 32),)),
        "w_out": noise(keys[6], (D, D), D ** -0.5, 0.09375, ((0, 32),)),
        "cache_keys": draw_cache_keys(jax.random.fold_in(keys[9], 71), 0),
        "cache_values": noise(keys[8], (STREAMS, CTX, D), 4.0, 24.0, ((1, 8), (2, 32))),
    }


epsilon = 1e-05
logit_gain = 2.0

def rotate(vector, positions):
    half_size = vector.shape[-1] // 2
    frequency = 10000.0 ** (-(jnp.arange(half_size, dtype=jnp.float32) * 2.0 / vector.shape[-1]))
    angles = positions.astype(jnp.float32)[..., None] * frequency
    cosine_term = jnp.cos(angles)[:, :, None, :]
    sine_term = jnp.sin(angles)[:, :, None, :]
    first_half = vector[..., :half_size]
    second_half = vector[..., half_size:]
    return jnp.concatenate([first_half * cosine_term - second_half * sine_term, first_half * sine_term + second_half * cosine_term], -1)

def reference(token_ids, cache_lengths, embed_table, attn_gain, final_gain, w_qkv, w_out, cache_keys, cache_values):
    heads = D // HD
    streams = token_ids.shape[1]
    embedded = embed_table[token_ids]
    embed_float = embedded.astype(jnp.float32)
    normed = (embed_float * lax.rsqrt(lax.optimization_barrier(jnp.mean(embed_float * embed_float, -1, keepdims=True)) + epsilon) * attn_gain).astype(jnp.bfloat16)
    projected = jnp.einsum('sbd,dcf->sbcf', normed.astype(jnp.float32), w_qkv.astype(jnp.float32), precision=lax.Precision.HIGHEST)
    head_shape = (2, streams, heads, HD)
    positions = cache_lengths[None, :] + jnp.arange(2, dtype=jnp.int32)[:, None]
    queries = rotate(projected[:, :, 0].reshape(head_shape), positions).astype(jnp.bfloat16)
    new_keys = rotate(projected[:, :, 1].reshape(head_shape), positions).astype(jnp.bfloat16)
    new_values = projected[:, :, 2].reshape(head_shape).astype(jnp.bfloat16)
    new_kv = jnp.stack([new_keys.reshape(2, streams, D), new_values.reshape(2, streams, D)])
    inverse = HD ** (-0.5)
    allowed = (jnp.arange(2)[None, :] <= jnp.arange(2)[:, None])[:, None, :]

    def attend_stream(packed):
        query_rows, key_rows, value_rows, length, fresh_keys, fresh_values = packed
        key_rows = key_rows.reshape(CTX, heads, HD).astype(jnp.float32)
        value_rows = value_rows.reshape(CTX, heads, HD).astype(jnp.float32)
        query_float = query_rows.astype(jnp.float32)
        cached = jnp.einsum('she,jhe->shj', query_float, key_rows, precision=lax.Precision.HIGHEST) * inverse
        fresh = jnp.einsum('she,the->sht', query_float, fresh_keys.astype(jnp.float32), precision=lax.Precision.HIGHEST) * inverse
        visible = jnp.broadcast_to((jnp.arange(CTX) < length)[None, None, :], cached.shape)
        scores = jnp.concatenate([cached, fresh], -1)
        mask_all = jnp.concatenate([visible, jnp.broadcast_to(allowed, fresh.shape)], -1)
        highest = lax.optimization_barrier(jnp.max(jnp.where(mask_all, scores, -1e+30), -1, keepdims=True))
        weights = jnp.where(mask_all, jnp.exp(scores - highest), 0.0)
        all_values = jnp.concatenate([value_rows, fresh_values.astype(jnp.float32)], 0)
        numerator = jnp.einsum('shj,jhe->she', weights, all_values, precision=lax.Precision.HIGHEST)
        return numerator / lax.optimization_barrier(jnp.sum(weights, -1))[..., None]
    attended = lax.map(attend_stream, (jnp.transpose(queries, (1, 0, 2, 3)), cache_keys, cache_values, cache_lengths, jnp.transpose(new_keys, (1, 0, 2, 3)), jnp.transpose(new_values, (1, 0, 2, 3))))
    attended = jnp.transpose(attended, (1, 0, 2, 3)).astype(jnp.bfloat16).reshape(2 * streams, D)
    mixed_rows = jnp.dot(attended, w_out, preferred_element_type=jnp.float32).reshape(2, streams, D)
    hidden = (embed_float + mixed_rows).astype(jnp.bfloat16)
    hidden_float = hidden.astype(jnp.float32)
    factor = lax.rsqrt(lax.optimization_barrier(jnp.mean(hidden_float * hidden_float, -1)) + epsilon) * (logit_gain / jnp.sqrt(jnp.float32(D)))
    gated_rows = (hidden_float * final_gain).astype(jnp.bfloat16).reshape(2 * streams, D)
    logits = lax.dot_general(gated_rows, embed_table, (((1,), (1,)), ((), ())), preferred_element_type=jnp.float32)
    logits = logits * factor.reshape(2 * streams, 1)
    highest = lax.optimization_barrier(jnp.max(logits, -1, keepdims=True))
    logprobs = logits - (highest + jnp.log(lax.optimization_barrier(jnp.sum(jnp.exp(logits - highest), -1, keepdims=True))))
    return (hidden, new_kv, logprobs.reshape(2, streams, V))
```

```python
import math

import jax
import jax.numpy as jnp
from jax import lax
from jax.sharding import Mesh
from jax.sharding import PartitionSpec as P

HD = 128
SEQ = ("seq_0", "seq_1")
TENSOR = ("tensor_0", "tensor_1")
SEQ_TENSOR = ("seq_0", "seq_1", "tensor_0", "tensor_1")
EVERYONE = ("tensor_1", "tensor_0", "seq_0", "seq_1")


epsilon = 1e-05
logit_gain = 2.0


def from_everyone(value, axis):
    copies = jnp.broadcast_to(value, (lax.axis_size(axis), *value.shape))
    return lax.all_to_all(copies, axis, split_axis=0, concat_axis=0, tiled=True)


def of_everyone(value, axis):
    everything = from_everyone(value, axis)
    return jnp.sum(everything.astype(jnp.float32), axis=0)


def in_order(parts, dim):
    parts = jnp.moveaxis(parts, 0, dim)
    shape = parts.shape
    return parts.reshape(*shape[:dim], shape[dim] * shape[dim + 1], *shape[dim + 2 :])


def gather_directly(value, axis, dim):
    parts = from_everyone(value, axis)
    return in_order(parts, dim)


def gathered_once(value, axis):
    leaves = jax.tree.leaves(value)
    sequence = sorted(range(len(leaves)), key=lambda k: -leaves[k].size)
    width = (1, *leaves[sequence[0]].shape)[-1]
    lines = [
        jnp.pad(leaves[k].reshape(-1), (0, -leaves[k].size % width)).reshape(-1, width)
        for k in sequence
    ]
    both, at, found = (from_everyone(jnp.concatenate(lines), axis), 0, {})
    for k, line in zip(sequence, lines):
        share = both[:, at : at + len(line)].reshape(len(both), -1)
        found[k] = share[:, : leaves[k].size].reshape(-1, *leaves[k].shape)
        at += len(line)
    numbers = iter(range(len(leaves)))
    return jax.tree.map(lambda _: found[next(numbers)], value)


def folded_in_pairs(pieces, combine):
    while len(jax.tree.leaves(pieces)[0]) > 1:
        pieces = jax.vmap(combine)(
            *(jax.tree.map(lambda part: part[side::2], pieces) for side in (0, 1))
        )
    return jax.tree.map(lambda part: part[0], pieces)


def combined_all(value, axis, combine):
    pieces = gathered_once(value, axis)
    return folded_in_pairs(pieces, combine)


def split_up(value, dim, count):
    shape = value.shape
    parts = value.reshape(*shape[:dim], count, shape[dim] // count, *shape[dim + 1 :])
    return jnp.moveaxis(parts, dim, 0)


def summed_on_arrival(value, axis, dim):
    parts = split_up(value, dim, lax.axis_size(axis))
    arrived = lax.all_to_all(parts, axis, split_axis=0, concat_axis=0, tiled=True)
    return arrived.astype(jnp.float32).sum(axis=0)


def rotate(vector, positions):
    half_size = vector.shape[-1] // 2
    frequency = 10000.0 ** (-(jnp.arange(half_size, dtype=jnp.float32) * 2.0 / vector.shape[-1]))
    angles = positions.astype(jnp.float32)[..., None] * frequency
    cosine_term = jnp.cos(angles)[:, :, None, :]
    sine_term = jnp.sin(angles)[:, :, None, :]
    first_half = vector[..., :half_size]
    second_half = vector[..., half_size:]
    return jnp.concatenate(
        [
            first_half * cosine_term - second_half * sine_term,
            first_half * sine_term + second_half * cosine_term,
        ],
        -1,
    )


def joint(earlier, later):
    earlier_max, earlier_sum, earlier_out = earlier
    later_max, later_sum, later_out = later
    highest = jnp.maximum(earlier_max, later_max)
    earlier_scale = jnp.exp(earlier_max - highest)
    later_scale = jnp.exp(later_max - highest)
    return (
        highest,
        earlier_sum * earlier_scale + later_sum * later_scale,
        earlier_out * earlier_scale[..., None] + later_out * later_scale[..., None],
    )


def thirds(value):
    high = lax.reduce_precision(value, 8, 7)
    middle = lax.reduce_precision(value - high, 8, 7)
    return jnp.concatenate([high, middle, value - high - middle]).astype(jnp.bfloat16)


def body(
    token_ids,
    cache_lengths,
    embed_table,
    attn_gain,
    final_gain,
    w_qkv,
    w_out,
    cache_keys,
    cache_values,
):
    streams = token_ids.shape[1]
    rows = 2 * streams
    vocab_rows, local_width = embed_table.shape
    model_width = attn_gain.shape[0]
    heads_here = local_width // HD
    slot_count = cache_keys.shape[1]
    seq_index = lax.axis_index(SEQ)
    tensor_index = lax.axis_index(TENSOR)
    local_ids = token_ids - seq_index * vocab_rows
    inside = (local_ids >= 0) & (local_ids < vocab_rows)
    picked = embed_table[jnp.clip(local_ids, 0, vocab_rows - 1)]
    picked = jnp.where(inside[..., None], picked, jnp.zeros_like(picked))
    embed_local = of_everyone(picked.astype(jnp.float32).astype(jnp.bfloat16), SEQ).astype(
        jnp.float32
    )
    embed_whole = gather_directly(embed_local.astype(jnp.bfloat16), TENSOR, 2).astype(jnp.float32)
    normed = (
        embed_whole
        * lax.rsqrt(jnp.mean(embed_whole * embed_whole, -1, keepdims=True) + epsilon)
        * attn_gain
    ).astype(jnp.bfloat16)
    projected = jnp.einsum("sbd,dcf->sbcf", normed, w_qkv, preferred_element_type=jnp.float32)
    head_shape = (2, streams, heads_here, HD)
    positions = cache_lengths[None, :] + jnp.arange(2, dtype=jnp.int32)[:, None]
    queries = rotate(projected[:, :, 0].reshape(head_shape), positions).astype(jnp.bfloat16)
    new_keys = rotate(projected[:, :, 1].reshape(head_shape), positions).astype(jnp.bfloat16)
    new_values = projected[:, :, 2].reshape(head_shape).astype(jnp.bfloat16)
    new_kv = jnp.stack(
        [new_keys.reshape(2, streams, local_width), new_values.reshape(2, streams, local_width)]
    )
    inverse = HD ** (-0.5)
    key_rows = cache_keys.reshape(streams, slot_count, heads_here, HD)
    value_rows = cache_values.reshape(streams, slot_count, heads_here, HD)
    scores = (
        jnp.einsum("sbhe,bjhe->sbhj", queries, key_rows, preferred_element_type=jnp.float32)
        * inverse
    )
    slot_positions = seq_index * slot_count + jnp.arange(slot_count, dtype=jnp.int32)
    visible = (slot_positions[None, :] < cache_lengths[:, None])[None, :, None, :]
    local_max = jnp.max(jnp.where(visible, scores, -1e30), -1)
    weights = jnp.where(visible, jnp.exp(scores - local_max[..., None]), 0.0)
    local_sum = jnp.sum(weights, -1)
    local_out = jnp.einsum(
        "sbhj,bjhe->sbhe",
        weights,
        value_rows,
        preferred_element_type=jnp.float32,
        precision=lax.Precision.HIGHEST,
    )
    highest, cache_total, cache_out = combined_all((local_max, local_sum, local_out), SEQ, joint)
    fresh_scores = (
        jnp.einsum("sbhe,tbhe->sbht", queries, new_keys, preferred_element_type=jnp.float32)
        * inverse
    )
    allowed = (jnp.arange(2)[None, :] <= jnp.arange(2)[:, None])[:, None, None, :]
    fresh_max = jnp.max(jnp.where(allowed, fresh_scores, -1e30), -1)
    overall = jnp.maximum(highest, fresh_max)
    fresh_weights = jnp.where(allowed, jnp.exp(fresh_scores - overall[..., None]), 0.0)
    cache_scale = jnp.exp(highest - overall)
    denominator = cache_total * cache_scale + jnp.sum(fresh_weights, -1)
    numerator = cache_out * cache_scale[..., None] + jnp.einsum(
        "sbht,tbhe->sbhe",
        fresh_weights,
        new_values,
        preferred_element_type=jnp.float32,
        precision=lax.Precision.HIGHEST,
    )
    attended = (
        (numerator / denominator[..., None]).astype(jnp.bfloat16).reshape(2 * streams, local_width)
    )
    mixed_rows = jnp.dot(attended, w_out, preferred_element_type=jnp.float32).reshape(
        2, streams, model_width
    )
    mixed_local = summed_on_arrival(mixed_rows.astype(jnp.bfloat16), TENSOR, 2)
    hidden = (embed_local + mixed_local).astype(jnp.bfloat16)
    hidden_float = hidden.astype(jnp.float32)
    own_squares = jnp.sum(hidden_float * hidden_float, -1).reshape(rows)
    final_local = lax.dynamic_slice_in_dim(final_gain, tensor_index * local_width, local_width)
    gated_rows = (hidden_float * final_local).astype(jnp.bfloat16).reshape(rows, local_width)
    partial_logits = lax.dot_general(
        gated_rows, embed_table, (((1,), (1,)), ((), ())), preferred_element_type=jnp.float32
    ).astype(jnp.bfloat16)
    peers = lax.axis_size(TENSOR)
    share_width = vocab_rows // peers
    sent = jnp.moveaxis(partial_logits.reshape(rows, peers, share_width), 1, 0)
    extra = jnp.pad(thirds(own_squares).reshape(1, 1, -1), ((0, 0), (0, 0), (0, share_width - 3 * rows)))
    sent = jnp.concatenate([sent, jnp.broadcast_to(extra, (peers, 1, share_width))], 1)
    arrived = lax.all_to_all(sent, TENSOR, split_axis=0, concat_axis=0, tiled=True)
    summed = jnp.sum(arrived.astype(jnp.float32), axis=0)
    final_squares = jnp.sum(summed[rows, : 3 * rows].reshape(3, rows), axis=0)
    factor_rows = (
        lax.rsqrt(final_squares / model_width + epsilon) * (logit_gain / math.sqrt(model_width))
    ).reshape(rows, 1)
    shares = summed[:rows] * factor_rows
    share_max = jnp.max(shares, -1)
    share_sum = jnp.sum(jnp.exp(shares - share_max[:, None]), -1)
    line = jnp.concatenate(
        [jnp.pad(part, (0, 64 - rows)) for part in (share_max, share_sum)]
    ).reshape(1, 128)
    lines = from_everyone(line, EVERYONE)[:, 0]
    maxima, sums = lines[:, :rows], lines[:, 64 : 64 + rows]
    vocab_max = jnp.max(maxima, 0)
    vocab_sum = jnp.sum(sums * jnp.exp(maxima - vocab_max), 0)
    logprobs = shares - (vocab_max + jnp.log(vocab_sum))[:, None]
    return (hidden, new_kv, logprobs.reshape(2, streams, -1))


def solution(mesh):
    split = Mesh(mesh.devices.reshape(4, 2, 4, 8), ("seq_0", "seq_1", "tensor_0", "tensor_1"))
    placed = (
        P(),
        P(),
        P(SEQ, TENSOR),
        P(),
        P(),
        P(None, None, TENSOR),
        P(TENSOR, None),
        P(None, SEQ, TENSOR),
        P(None, SEQ, TENSOR),
    )
    return jax.shard_map(
        body,
        mesh=split,
        in_specs=placed,
        out_specs=(P(None, None, TENSOR), P(None, None, None, TENSOR), P(None, None, SEQ_TENSOR)),
        check_vma=False,
    )
```

```python
import functools
import math

import jax
import jax.numpy as jnp
from jax import lax
from jax.experimental import pallas as pl
from jax.experimental.pallas import tpu as pltpu
from jax.sharding import Mesh
from jax.sharding import PartitionSpec as P

HD = 128
TILE = 16
SEQ = ("seq_0", "seq_1")
TENSOR = ("tensor_0", "tensor_1")
SEQ_TENSOR = ("seq_0", "seq_1", "tensor_0", "tensor_1")
EVERYONE = ("tensor_1", "tensor_0", "seq_0", "seq_1")

epsilon = 1e-05
logit_gain = 2.0
lowest = -1e30
f32, bf16 = jnp.float32, jnp.bfloat16
VMEM = pl.BlockSpec(memory_space=pltpu.VMEM)
MIB = 1024 * 1024
PICK_GRANT = 61 * MIB
STAGE_GRANT = 49 * MIB + MIB // 2
ATTEND_GRANT = 51 * MIB + MIB // 2
HEAD_GRANT = 51 * MIB
ATTEND_CHUNKS = 8
IN_FLIGHT = 4
STAGED = 18
SMEM = pl.BlockSpec(memory_space=pltpu.SMEM)
HBM = pl.BlockSpec(memory_space=pltpu.HBM)


def exchange(copies, axis):
    return lax.all_to_all(copies, axis, split_axis=0, concat_axis=0, tiled=True)


def row_of(width=HD):
    return lax.broadcasted_iota(jnp.int32, (TILE, width), 0)


def lane_of(width=HD):
    return lax.broadcasted_iota(jnp.int32, (TILE, width), 1)


def as_line(column):
    return jnp.sum(jnp.where(row_of() == lane_of(), column, 0.0), 0, keepdims=True)


def as_column(line):
    return jnp.sum(jnp.where(row_of() == lane_of(), line, 0.0), 1, keepdims=True)


def pick_kernel(place, ids, table, out, groups, sems):
    streams = ids.shape[1]
    vocab_rows = table.shape[0]
    within, copies = [], []
    for row in range(2 * streams):
        local = ids[row // streams, row % streams] - place[0] * vocab_rows
        inside = (local >= 0) & (local < vocab_rows)
        local = jnp.clip(local, 0, vocab_rows - 1)
        offset = lax.rem(local, TILE)
        start = pl.multiple_of(local - offset, TILE)
        copy = pltpu.make_async_copy(table.at[pl.ds(start, TILE)], groups.at[row], sems.at[row])
        copy.start()
        copies.append(copy)
        within.append(jnp.where(inside, offset, TILE))
    total = jnp.zeros((TILE, HD), f32)
    for row, copy in enumerate(copies):
        copy.wait()
        block = groups[row].astype(f32)
        found = jnp.sum(jnp.where(row_of() == within[row], block, 0.0), 0, keepdims=True)
        total = jnp.where(row_of() == row, found, total)
    picked = total.astype(bf16)
    for peer in range(out.shape[0]):
        out[peer] = picked


class Stream:
    def __init__(self, copies):
        self.copies, self.begun, self.done = copies, 0, 0
        for _ in range(min(IN_FLIGHT, len(copies))):
            self.begin()

    def begin(self):
        if self.begun < len(self.copies):
            self.copies[self.begun].start()
            self.begun += 1

    def wait(self):
        self.copies[self.done].wait()
        self.done += 1
        self.begin()


def stage_kernel(after, table, out, sems):
    del after
    chunks = sems.shape[0]
    tall = out.shape[0] // chunks
    copies = [
        pltpu.make_async_copy(
            table.at[pl.ds(k * tall, tall)], out.at[pl.ds(k * tall, tall)], sems.at[k]
        )
        for k in range(chunks)
    ]
    for copy in copies:
        copy.start()
    for copy in copies:
        copy.wait()


def attend_kernel(
    place,
    lengths,
    gathered,
    gain,
    cosine,
    sine,
    keys,
    all_w_qkv,
    all_values,
    out,
    new_kv,
    w_qkv,
    values,
    weight_sems,
    value_sems,
):
    streams, slots, _ = keys.shape
    chunks = weight_sems.shape[0]
    tall = w_qkv.shape[1] // chunks
    weight_copies = [
        pltpu.make_async_copy(
            all_w_qkv.at[:, pl.ds(k * tall, tall)], w_qkv.at[:, pl.ds(k * tall, tall)], weight_sems.at[k]
        )
        for k in range(chunks)
    ]
    value_copies = [
        pltpu.make_async_copy(all_values.at[b], values.at[b], value_sems.at[b])
        for b in range(streams)
    ]
    arrivals = Stream(weight_copies + value_copies)
    blocks = gathered.shape[0]
    width = blocks * HD
    seq = place[0]
    squares = jnp.zeros((TILE, HD), f32)
    for k in range(blocks):
        part = gathered[k].astype(f32)
        squares = squares + part * part
    scale = lax.rsqrt(jnp.sum(squares, 1, keepdims=True) / width + epsilon)
    normed = [
        (gathered[k].astype(f32) * scale * gain[k : k + 1]).astype(bf16) for k in range(blocks)
    ]
    per = blocks // chunks
    projected = [jnp.zeros((TILE, HD), f32)] * 3
    for k in range(chunks):
        some = jnp.concatenate(normed[k * per : (k + 1) * per], 1)
        arrivals.wait()
        projected = [
            total
            + jnp.dot(some, w_qkv[c, k * tall : (k + 1) * tall, :], preferred_element_type=f32)
            for c, total in enumerate(projected)
        ]
    query, key, value = projected

    def rotated(part):
        return (part * cosine[...] + pltpu.roll(part, HD // 2, 1) * sine[...]).astype(bf16)

    query, key, value = rotated(query), rotated(key), value.astype(bf16)
    new_kv[0] = key
    new_kv[1] = value

    inverse = HD ** (-0.5)
    over_lanes = (((1,), (1,)), ((), ()))
    rows = row_of(slots)
    scores = jnp.zeros((TILE, slots), f32)
    length = jnp.zeros((TILE, slots), jnp.int32)
    for b in range(streams):
        mine = (rows == b) | (rows == streams + b)
        some = lax.dot_general(query, keys[b], over_lanes, preferred_element_type=f32)
        scores = jnp.where(mine, some, scores)
        length = jnp.where(mine, lengths[b], length)
    visible = lane_of(slots) + seq * slots < length
    scores = jnp.where(visible, scores * inverse, lowest)

    row, lane = row_of(TILE), lane_of(TILE)
    step, lane_step = (row >= streams).astype(jnp.int32), (lane >= streams).astype(jnp.int32)
    allowed = (row - step * streams == lane - lane_step * streams) & (lane_step <= step)
    allowed = allowed & (row < 2 * streams) & (lane < 2 * streams) & (seq == 0)
    fresh = lax.dot_general(query, key, over_lanes, preferred_element_type=f32)
    fresh = jnp.where(allowed, fresh * inverse, lowest)

    highest = jnp.maximum(jnp.max(scores, 1, keepdims=True), jnp.max(fresh, 1, keepdims=True))
    weights = jnp.where(visible, jnp.exp(scores - highest), 0.0)
    fresh_weights = jnp.where(allowed, jnp.exp(fresh - highest), 0.0)
    total = jnp.sum(weights, 1, keepdims=True) + jnp.sum(fresh_weights, 1, keepdims=True)
    mixed = jnp.dot(fresh_weights.astype(bf16), value, preferred_element_type=f32)
    for b in range(streams):
        mine = (rows == b) | (rows == streams + b)
        share = jnp.where(mine, weights, 0.0).astype(bf16)
        arrivals.wait()
        mixed = mixed + jnp.dot(share, values[b], preferred_element_type=f32)
    sent = jnp.where(row_of() == TILE - 2, as_line(highest), mixed)
    sent = jnp.where(row_of() == TILE - 1, as_line(total), sent)
    for peer in range(out.shape[0]):
        out[peer] = sent


def merge_kernel(rows, parts, w_out, out):
    count = parts.shape[0]
    peaks = [as_column(parts[k, TILE - 2 : TILE - 1, :]) for k in range(count)]
    highest = functools.reduce(jnp.maximum, peaks)
    numerator = jnp.zeros((TILE, HD), f32)
    denominator = jnp.zeros((TILE, 1), f32)
    for k in range(count):
        scale = jnp.exp(peaks[k] - highest)
        numerator = numerator + parts[k] * scale
        denominator = denominator + as_column(parts[k, TILE - 1 : TILE, :]) * scale
    real = row_of() < rows
    attended = jnp.where(real, numerator / jnp.where(real, denominator, 1.0), 0.0).astype(bf16)
    per = 8
    for group in range(out.shape[0] // per):
        some = jnp.dot(
            attended, w_out[:, group * per * HD : (group + 1) * per * HD], preferred_element_type=f32
        ).astype(bf16)
        for k in range(per):
            out[group * per + k] = some[:, k * HD : (k + 1) * HD]


def head_kernel(parts, embedded, gain, staged, whole_table, hidden_out, out, table, sems):
    peers, _, share = out.shape
    first = staged.shape[0] // share
    chunks = sems.shape[0]
    tall = table.shape[0] // chunks
    arrivals = Stream(
        [
            pltpu.make_async_copy(
                whole_table.at[pl.ds(first * share + k * tall, tall)],
                table.at[pl.ds(k * tall, tall)],
                sems.at[k],
            )
            for k in range(chunks)
        ]
    )
    mixed = jnp.zeros((TILE, HD), f32)
    for k in range(parts.shape[0]):
        mixed = mixed + parts[k].astype(f32)
    hidden = (embedded[...].astype(f32) + mixed).astype(bf16)
    hidden_out[...] = hidden
    wide = hidden.astype(f32)
    squares = as_line(jnp.sum(wide * wide, 1, keepdims=True))
    high = squares.astype(bf16).astype(f32)
    middle = (squares - high).astype(bf16).astype(f32)
    low = squares - high - middle
    line = jnp.concatenate([high, middle, low, jnp.zeros((1, share - 3 * HD), f32)], 1)
    gated = (wide * gain[...]).astype(bf16)
    spare = row_of(share) == TILE - 1
    for k in range(peers):
        source, at = (staged, k) if k < first else (table, k - first)
        if k >= first and at % (tall // share) == 0:
            arrivals.wait()
        some = lax.dot_general(
            gated,
            source[at * share : (at + 1) * share, :],
            (((1,), (1,)), ((), ())),
            preferred_element_type=f32,
        )
        out[k] = jnp.where(spare, line, some).astype(bf16)


def body(
    token_ids,
    cache_lengths,
    embed_table,
    attn_gain,
    final_gain,
    w_qkv,
    w_out,
    cache_keys,
    cache_values,
):
    streams = token_ids.shape[1]
    rows = 2 * streams
    vocab_rows, local_width = embed_table.shape
    model_width = attn_gain.shape[0]
    seqs, peers = lax.axis_size(SEQ), lax.axis_size(TENSOR)
    tensor_index = lax.axis_index(TENSOR)
    place = lax.axis_index(SEQ).astype(jnp.int32).reshape(1)
    params = pltpu.CompilerParams(vmem_limit_bytes=16 * 1024 * 1024)
    shape = jax.ShapeDtypeStruct

    picked = pl.pallas_call(
        pick_kernel,
        out_shape=shape((seqs, TILE, HD), bf16),
        in_specs=[SMEM, SMEM, HBM],
        out_specs=VMEM,
        scratch_shapes=[
            pltpu.VMEM((rows, TILE, HD), bf16),
            pltpu.SemaphoreType.DMA((rows,)),
        ],
        compiler_params=pltpu.CompilerParams(vmem_limit_bytes=PICK_GRANT),
        cost_estimate=pl.CostEstimate(flops=0, bytes_accessed=2**17, transcendentals=0),
        name="pick",
    )(place, token_ids, embed_table)
    embedded = jnp.sum(exchange(picked, SEQ).astype(f32), 0).astype(bf16)
    gathered = exchange(jnp.broadcast_to(embedded, (peers, TILE, HD)), TENSOR)

    positions = (cache_lengths[None, :] + jnp.arange(2, dtype=jnp.int32)[:, None]).reshape(rows)
    half = HD // 2
    frequency = 10000.0 ** (-(jnp.arange(half, dtype=f32) * 2.0 / HD))
    angles = positions.astype(f32)[:, None] * frequency
    cosine, sine = jnp.cos(angles), jnp.sin(angles)
    padding = ((0, TILE - rows), (0, 0))
    cosine = jnp.pad(jnp.concatenate([cosine, cosine], 1), padding)
    sine = jnp.pad(jnp.concatenate([-sine, sine], 1), padding)

    parts, new_kv = pl.pallas_call(
        attend_kernel,
        out_shape=(shape((seqs, TILE, HD), f32), shape((2, TILE, HD), bf16)),
        in_specs=[SMEM, SMEM] + [VMEM] * 5 + [HBM] * 2,
        out_specs=(VMEM, VMEM),
        scratch_shapes=[
            pltpu.VMEM((3, model_width, HD), bf16),
            pltpu.VMEM(cache_values.shape, bf16),
            pltpu.SemaphoreType.DMA((ATTEND_CHUNKS,)),
            pltpu.SemaphoreType.DMA((streams,)),
        ],
        compiler_params=pltpu.CompilerParams(vmem_limit_bytes=ATTEND_GRANT),
        name="attend",
    )(
        place,
        cache_lengths,
        gathered,
        attn_gain.reshape(peers, HD),
        cosine,
        sine,
        cache_keys,
        jnp.moveaxis(w_qkv, 1, 0),
        cache_values,
    )
    mixed = pl.pallas_call(
        functools.partial(merge_kernel, rows),
        out_shape=shape((peers, TILE, HD), bf16),
        in_specs=[VMEM, VMEM],
        out_specs=VMEM,
        compiler_params=params,
        name="merge",
    )(exchange(parts, SEQ), w_out)
    share_width = vocab_rows // peers
    staged_rows = STAGED * peers // 32 * share_width
    staged = pl.pallas_call(
        stage_kernel,
        out_shape=shape((staged_rows, HD), bf16),
        in_specs=[HBM, HBM],
        out_specs=VMEM,
        scratch_shapes=[pltpu.SemaphoreType.DMA((6,))],
        compiler_params=pltpu.CompilerParams(vmem_limit_bytes=STAGE_GRANT),
        cost_estimate=pl.CostEstimate(
            flops=0, bytes_accessed=4 * HD * staged_rows, transcendentals=0
        ),
        name="stage",
    )(mixed, embed_table)
    hidden, sent = pl.pallas_call(
        head_kernel,
        out_shape=(shape((TILE, HD), bf16), shape((peers, TILE, share_width), bf16)),
        in_specs=[VMEM] * 4 + [HBM],
        out_specs=(VMEM, VMEM),
        scratch_shapes=[
            pltpu.VMEM((vocab_rows - staged_rows, HD), bf16),
            pltpu.SemaphoreType.DMA(((vocab_rows - staged_rows) // (2 * share_width),)),
        ],
        compiler_params=pltpu.CompilerParams(vmem_limit_bytes=HEAD_GRANT),
        name="head",
    )(
        exchange(mixed, TENSOR),
        embedded,
        lax.dynamic_slice_in_dim(final_gain, tensor_index * HD, HD).reshape(1, HD),
        staged,
        embed_table,
    )
    summed = jnp.sum(exchange(sent, TENSOR).astype(f32), axis=0)
    line = summed[TILE - 1, : 3 * HD].reshape(3, HD)[:, :rows]
    final_squares = jnp.sum(line, axis=0)
    factor_rows = (
        lax.rsqrt(final_squares / model_width + epsilon) * (logit_gain / math.sqrt(model_width))
    ).reshape(rows, 1)
    shares = summed[:rows] * factor_rows
    share_max = jnp.max(shares, -1)
    share_sum = jnp.sum(jnp.exp(shares - share_max[:, None]), -1)
    line = jnp.concatenate(
        [jnp.pad(part, (0, HD // 2 - rows)) for part in (share_max, share_sum)]
    ).reshape(1, HD)
    everyone = seqs * peers
    lines = exchange(jnp.broadcast_to(line, (everyone, 1, HD)), EVERYONE)[:, 0]
    maxima, sums = lines[:, :rows], lines[:, HD // 2 : HD // 2 + rows]
    vocab_max = jnp.max(maxima, 0)
    vocab_sum = jnp.sum(sums * jnp.exp(maxima - vocab_max), 0)
    logprobs = shares - (vocab_max + jnp.log(vocab_sum))[:, None]
    return (
        hidden[:rows].reshape(2, streams, local_width),
        new_kv[:, :rows].reshape(2, 2, streams, local_width),
        logprobs.reshape(2, streams, -1),
    )


def solution(mesh):
    split = Mesh(mesh.devices.reshape(4, 2, 4, 8), ("seq_0", "seq_1", "tensor_0", "tensor_1"))
    placed = (
        P(),
        P(),
        P(SEQ, TENSOR),
        P(),
        P(),
        P(None, None, TENSOR),
        P(TENSOR, None),
        P(None, SEQ, TENSOR),
        P(None, SEQ, TENSOR),
    )
    return jax.shard_map(
        body,
        mesh=split,
        in_specs=placed,
        out_specs=(P(None, None, TENSOR), P(None, None, None, TENSOR), P(None, None, SEQ_TENSOR)),
        check_vma=False,
    )
```

```python
import functools
import math

import jax
import jax.numpy as jnp
from jax import lax
from jax.experimental import pallas as pl
from jax.experimental.pallas import tpu as pltpu
from jax.sharding import Mesh
from jax.sharding import PartitionSpec as P

HD = 128
TILE = 16
SEQ = ("seq_0", "seq_1")
TENSOR = ("tensor_0", "tensor_1")
SEQ_TENSOR = ("seq_0", "seq_1", "tensor_0", "tensor_1")
EVERYONE = ("tensor_1", "tensor_0", "seq_0", "seq_1")

epsilon = 1e-05
logit_gain = 2.0
lowest = -1e30
f32, bf16 = jnp.float32, jnp.bfloat16
VMEM = pl.BlockSpec(memory_space=pltpu.VMEM)
MIB = 1024 * 1024
PICK_GRANT = 61 * MIB
STAGE_GRANT = 49 * MIB + MIB // 2
ATTEND_GRANT = 206 * MIB // 4
HEAD_GRANT = 202 * MIB // 4
W_STAGED = 16
STAGED = 22
SMEM = pl.BlockSpec(memory_space=pltpu.SMEM)
HBM = pl.BlockSpec(memory_space=pltpu.HBM)


def exchange(copies, axis):
    return lax.all_to_all(copies, axis, split_axis=0, concat_axis=0, tiled=True)


def row_of(width=HD):
    return lax.broadcasted_iota(jnp.int32, (TILE, width), 0)


def lane_of(width=HD):
    return lax.broadcasted_iota(jnp.int32, (TILE, width), 1)


def as_line(column):
    return jnp.sum(jnp.where(row_of() == lane_of(), column, 0.0), 0, keepdims=True)


def as_column(line):
    return jnp.sum(jnp.where(row_of() == lane_of(), line, 0.0), 1, keepdims=True)


def pick_kernel(place, ids, table, out, groups, sems):
    streams = ids.shape[1]
    vocab_rows = table.shape[0]
    within, copies = [], []
    for row in range(2 * streams):
        local = ids[row // streams, row % streams] - place[0] * vocab_rows
        inside = (local >= 0) & (local < vocab_rows)
        local = jnp.clip(local, 0, vocab_rows - 1)
        offset = lax.rem(local, TILE)
        start = pl.multiple_of(local - offset, TILE)
        copy = pltpu.make_async_copy(table.at[pl.ds(start, TILE)], groups.at[row], sems.at[row])
        copy.start()
        copies.append(copy)
        within.append(jnp.where(inside, offset, TILE))
    total = jnp.zeros((TILE, HD), f32)
    for row, copy in enumerate(copies):
        copy.wait()
        block = groups[row].astype(f32)
        found = jnp.sum(jnp.where(row_of() == within[row], block, 0.0), 0, keepdims=True)
        total = jnp.where(row_of() == row, found, total)
    picked = total.astype(bf16)
    for peer in range(out.shape[0]):
        out[peer] = picked


def stage_kernel(after, source, out, sems):
    del after
    lead = (slice(None),) * (len(source.shape) - 2)
    chunks = sems.shape[0]
    tall = out.shape[-2] // chunks
    copies = []
    for k in range(chunks):
        part = (*lead, pl.ds(k * tall, tall))
        copies.append(pltpu.make_async_copy(source.at[part], out.at[part], sems.at[k]))
        copies[-1].start()
    for copy in copies:
        copy.wait()


def staged(after, source, rows):
    shape = (*source.shape[:-2], rows, source.shape[-1])
    return pl.pallas_call(
        stage_kernel,
        out_shape=jax.ShapeDtypeStruct(shape, source.dtype),
        in_specs=[HBM, HBM],
        out_specs=VMEM,
        scratch_shapes=[pltpu.SemaphoreType.DMA((4,))],
        compiler_params=pltpu.CompilerParams(vmem_limit_bytes=STAGE_GRANT),
        cost_estimate=pl.CostEstimate(
            flops=0, bytes_accessed=4 * math.prod(shape), transcendentals=0
        ),
        name="stage",
    )(after, source)


def attend_kernel(
    place,
    lengths,
    gathered,
    gain,
    cosine,
    sine,
    w_start,
    all_w_qkv,
    all_keys,
    all_values,
    out,
    new_kv,
    w_rest,
    keys,
    values,
    sems,
):
    streams, slots, _ = keys.shape
    first = w_start.shape[1]
    weight_copy = pltpu.make_async_copy(
        all_w_qkv.at[:, pl.ds(first, w_rest.shape[1])], w_rest, sems.at[0]
    )
    key_copy = pltpu.make_async_copy(all_keys, keys, sems.at[1])
    value_copy = pltpu.make_async_copy(all_values, values, sems.at[2])
    for copy in (weight_copy, key_copy, value_copy):
        copy.start()
    blocks = gathered.shape[0]
    width = blocks * HD
    seq = place[0]
    squares = jnp.zeros((TILE, HD), f32)
    for k in range(blocks):
        part = gathered[k].astype(f32)
        squares = squares + part * part
    scale = lax.rsqrt(jnp.sum(squares, 1, keepdims=True) / width + epsilon)
    normed = [
        (gathered[k].astype(f32) * scale * gain[k : k + 1]).astype(bf16) for k in range(blocks)
    ]
    begin = jnp.concatenate(normed[: first // HD], 1)
    rest = jnp.concatenate(normed[first // HD :], 1)
    query, key, value = (
        jnp.dot(begin, w_start[c], preferred_element_type=f32) for c in range(3)
    )
    weight_copy.wait()
    query, key, value = (
        total + jnp.dot(rest, w_rest[c], preferred_element_type=f32)
        for c, total in enumerate((query, key, value))
    )

    def rotated(part):
        return (part * cosine[...] + pltpu.roll(part, HD // 2, 1) * sine[...]).astype(bf16)

    query, key, value = rotated(query), rotated(key), value.astype(bf16)
    new_kv[0] = key
    new_kv[1] = value

    inverse = HD ** (-0.5)
    over_lanes = (((1,), (1,)), ((), ()))
    rows = row_of(slots)
    scores = jnp.zeros((TILE, slots), f32)
    length = jnp.zeros((TILE, 1), jnp.int32)
    first_lane = row_of(1)
    key_copy.wait()
    for b in range(streams):
        mine = (rows == b) | (rows == streams + b)
        some = lax.dot_general(query, keys[b], over_lanes, preferred_element_type=f32)
        scores = jnp.where(mine, some, scores)
        length = jnp.where(
            (first_lane == b) | (first_lane == streams + b), lengths[b], length
        )
    visible = lane_of(slots) + seq * slots < length
    scores = jnp.where(visible, scores * inverse, lowest)

    row, lane = row_of(TILE), lane_of(TILE)
    step, lane_step = (row >= streams).astype(jnp.int32), (lane >= streams).astype(jnp.int32)
    allowed = (row - step * streams == lane - lane_step * streams) & (lane_step <= step)
    allowed = allowed & (row < 2 * streams) & (lane < 2 * streams) & (seq == 0)
    fresh = lax.dot_general(query, key, over_lanes, preferred_element_type=f32)
    fresh = jnp.where(allowed, fresh * inverse, lowest)

    highest = jnp.maximum(jnp.max(scores, 1, keepdims=True), jnp.max(fresh, 1, keepdims=True))
    weights = jnp.where(visible, jnp.exp(scores - highest), 0.0)
    fresh_weights = jnp.where(allowed, jnp.exp(fresh - highest), 0.0)
    total = jnp.sum(weights, 1, keepdims=True) + jnp.sum(fresh_weights, 1, keepdims=True)
    mixed = jnp.dot(fresh_weights.astype(bf16), value, preferred_element_type=f32)
    value_copy.wait()
    for b in range(streams):
        mine = (rows == b) | (rows == streams + b)
        share = jnp.where(mine, weights, 0.0).astype(bf16)
        mixed = mixed + jnp.dot(share, values[b], preferred_element_type=f32)
    sent = jnp.where(row_of() == TILE - 2, as_line(highest), mixed)
    sent = jnp.where(row_of() == TILE - 1, as_line(total), sent)
    for peer in range(out.shape[0]):
        out[peer] = sent


def merge_kernel(rows, parts, w_out, out):
    count = parts.shape[0]
    peaks = [as_column(parts[k, TILE - 2 : TILE - 1, :]) for k in range(count)]
    highest = functools.reduce(jnp.maximum, peaks)
    numerator = jnp.zeros((TILE, HD), f32)
    denominator = jnp.zeros((TILE, 1), f32)
    for k in range(count):
        scale = jnp.exp(peaks[k] - highest)
        numerator = numerator + parts[k] * scale
        denominator = denominator + as_column(parts[k, TILE - 1 : TILE, :]) * scale
    real = row_of() < rows
    attended = jnp.where(real, numerator / jnp.where(real, denominator, 1.0), 0.0).astype(bf16)
    per = 8
    for group in range(out.shape[0] // per):
        some = jnp.dot(
            attended, w_out[:, group * per * HD : (group + 1) * per * HD], preferred_element_type=f32
        ).astype(bf16)
        for k in range(per):
            out[group * per + k] = some[:, k * HD : (k + 1) * HD]


def head_kernel(parts, embedded, gain, staged, whole_table, hidden_out, out, table, sem):
    peers, _, share = out.shape
    first = staged.shape[0] // share
    rest = pltpu.make_async_copy(
        whole_table.at[pl.ds(first * share, table.shape[0])], table, sem
    )
    rest.start()
    mixed = jnp.zeros((TILE, HD), f32)
    for k in range(parts.shape[0]):
        mixed = mixed + parts[k].astype(f32)
    hidden = (embedded[...].astype(f32) + mixed).astype(bf16)
    hidden_out[...] = hidden
    wide = hidden.astype(f32)
    squares = as_line(jnp.sum(wide * wide, 1, keepdims=True))
    high = squares.astype(bf16).astype(f32)
    middle = (squares - high).astype(bf16).astype(f32)
    low = squares - high - middle
    line = jnp.concatenate([high, middle, low, jnp.zeros((1, share - 3 * HD), f32)], 1)
    gated = (wide * gain[...]).astype(bf16)
    spare = row_of(share) == TILE - 1
    for k in range(peers):
        source, at = (staged, k) if k < first else (table, k - first)
        if k == first:
            rest.wait()
        some = lax.dot_general(
            gated,
            source[at * share : (at + 1) * share, :],
            (((1,), (1,)), ((), ())),
            preferred_element_type=f32,
        )
        out[k] = jnp.where(spare, line, some).astype(bf16)


def share_kernel(model_width, parts, shares_out, lines_out):
    total = parts[0].astype(f32)
    for k in range(1, parts.shape[0]):
        total = total + parts[k].astype(f32)
    line = total[TILE - 1 :, :]
    squares = as_column(line[:, :HD] + line[:, HD : 2 * HD] + line[:, 2 * HD : 3 * HD])
    factor = lax.rsqrt(squares / model_width + epsilon) * (logit_gain / math.sqrt(model_width))
    shares = total * factor
    shares_out[...] = shares
    highest = jnp.max(shares, 1, keepdims=True)
    summed = jnp.sum(jnp.exp(shares - highest), 1, keepdims=True)
    sent = as_line(highest) + pltpu.roll(as_line(summed), HD // 2, 1)
    lines_out[...] = jnp.broadcast_to(sent.reshape(1, 1, HD), lines_out.shape)


def finish_kernel(shares, lines, out):
    every = lines[...]
    highest = jnp.max(every, 0, keepdims=True)
    scaled = pltpu.roll(every, HD // 2, 2) * jnp.exp(every - highest)
    summed = jnp.sum(scaled, 0)
    lane = lax.broadcasted_iota(jnp.int32, summed.shape, 1)
    summed = jnp.where(lane < TILE, summed, 1.0)
    total = as_column(highest[0] + jnp.log(summed))
    logprobs = shares[...] - total
    streams = out.shape[0]
    for b in range(streams):
        out[b, 0:1, :] = logprobs[b : b + 1, :]
        out[b, 1:2, :] = logprobs[streams + b : streams + b + 1, :]


def body(
    token_ids,
    cache_lengths,
    embed_table,
    attn_gain,
    final_gain,
    w_qkv,
    w_out,
    cache_keys,
    cache_values,
):
    streams = token_ids.shape[1]
    rows = 2 * streams
    vocab_rows, local_width = embed_table.shape
    model_width = attn_gain.shape[0]
    seqs, peers = lax.axis_size(SEQ), lax.axis_size(TENSOR)
    tensor_index = lax.axis_index(TENSOR)
    place = lax.axis_index(SEQ).astype(jnp.int32).reshape(1)
    params = pltpu.CompilerParams(vmem_limit_bytes=16 * 1024 * 1024)
    shape = jax.ShapeDtypeStruct

    picked = pl.pallas_call(
        pick_kernel,
        out_shape=shape((seqs, TILE, HD), bf16),
        in_specs=[SMEM, SMEM, HBM],
        out_specs=VMEM,
        scratch_shapes=[
            pltpu.VMEM((rows, TILE, HD), bf16),
            pltpu.SemaphoreType.DMA((rows,)),
        ],
        compiler_params=pltpu.CompilerParams(vmem_limit_bytes=PICK_GRANT),
        cost_estimate=pl.CostEstimate(flops=0, bytes_accessed=2**17, transcendentals=0),
        name="pick",
    )(place, token_ids, embed_table)
    embedded = jnp.sum(exchange(picked, SEQ).astype(f32), 0).astype(bf16)
    gathered = exchange(jnp.broadcast_to(embedded, (peers, TILE, HD)), TENSOR)

    positions = (cache_lengths[None, :] + jnp.arange(2, dtype=jnp.int32)[:, None]).reshape(rows)
    half = HD // 2
    frequency = 10000.0 ** (-(jnp.arange(half, dtype=f32) * 2.0 / HD))
    angles = positions.astype(f32)[:, None] * frequency
    cosine, sine = jnp.cos(angles), jnp.sin(angles)
    padding = ((0, TILE - rows), (0, 0))
    cosine = jnp.pad(jnp.concatenate([cosine, cosine], 1), padding)
    sine = jnp.pad(jnp.concatenate([-sine, sine], 1), padding)

    w_qkv = jnp.moveaxis(w_qkv, 1, 0)
    w_rows = model_width * W_STAGED // 32
    parts, new_kv = pl.pallas_call(
        attend_kernel,
        out_shape=(shape((seqs, TILE, HD), f32), shape((2, TILE, HD), bf16)),
        in_specs=[SMEM, SMEM] + [VMEM] * 5 + [HBM] * 3,
        out_specs=(VMEM, VMEM),
        scratch_shapes=[
            pltpu.VMEM((3, model_width - w_rows, HD), bf16),
            pltpu.VMEM(cache_keys.shape, bf16),
            pltpu.VMEM(cache_values.shape, bf16),
            pltpu.SemaphoreType.DMA((3,)),
        ],
        compiler_params=pltpu.CompilerParams(vmem_limit_bytes=ATTEND_GRANT),
        name="attend",
    )(
        place,
        cache_lengths,
        gathered,
        attn_gain.reshape(peers, HD),
        cosine,
        sine,
        staged(embedded, w_qkv, w_rows),
        w_qkv,
        cache_keys,
        cache_values,
    )
    mixed = pl.pallas_call(
        functools.partial(merge_kernel, rows),
        out_shape=shape((peers, TILE, HD), bf16),
        in_specs=[VMEM, VMEM],
        out_specs=VMEM,
        compiler_params=params,
        name="merge",
    )(exchange(parts, SEQ), w_out)
    share_width = vocab_rows // peers
    staged_rows = STAGED * peers // 32 * share_width
    table_start = staged(mixed, embed_table, staged_rows)
    hidden, sent = pl.pallas_call(
        head_kernel,
        out_shape=(shape((TILE, HD), bf16), shape((peers, TILE, share_width), bf16)),
        in_specs=[VMEM] * 4 + [HBM],
        out_specs=(VMEM, VMEM),
        scratch_shapes=[
            pltpu.VMEM((vocab_rows - staged_rows, HD), bf16),
            pltpu.SemaphoreType.DMA,
        ],
        compiler_params=pltpu.CompilerParams(vmem_limit_bytes=HEAD_GRANT),
        name="head",
    )(
        exchange(mixed, TENSOR),
        embedded,
        lax.dynamic_slice_in_dim(final_gain, tensor_index * HD, HD).reshape(1, HD),
        table_start,
        embed_table,
    )
    everyone = seqs * peers
    shares, lines = pl.pallas_call(
        functools.partial(share_kernel, model_width),
        out_shape=(shape((TILE, share_width), f32), shape((everyone, 1, HD), f32)),
        in_specs=[VMEM],
        out_specs=(VMEM, VMEM),
        compiler_params=params,
        name="share",
    )(exchange(sent, TENSOR))
    logprobs = pl.pallas_call(
        finish_kernel,
        out_shape=shape((streams, 2, share_width), f32),
        in_specs=[VMEM, VMEM],
        out_specs=VMEM,
        compiler_params=params,
        name="finish",
    )(shares, exchange(lines, EVERYONE))
    return (
        hidden[:rows].reshape(2, streams, local_width),
        new_kv[:, :rows].reshape(2, 2, streams, local_width),
        jnp.swapaxes(logprobs, 0, 1),
    )


def solution(mesh):
    split = Mesh(mesh.devices.reshape(4, 2, 4, 8), ("seq_0", "seq_1", "tensor_0", "tensor_1"))
    placed = (
        P(),
        P(),
        P(SEQ, TENSOR),
        P(),
        P(),
        P(None, None, TENSOR),
        P(TENSOR, None),
        P(None, SEQ, TENSOR),
        P(None, SEQ, TENSOR),
    )
    return jax.shard_map(
        body,
        mesh=split,
        in_specs=placed,
        out_specs=(P(None, None, TENSOR), P(None, None, None, TENSOR), P(None, None, SEQ_TENSOR)),
        check_vma=False,
    )
```

```python
import functools
import math

import jax
import jax.numpy as jnp
from jax import lax
from jax.experimental import pallas as pl
from jax.experimental.pallas import tpu as pltpu
from jax.sharding import Mesh
from jax.sharding import PartitionSpec as P

HD = 128
TILE = 16
SEQ = ("seq_0", "seq_1")
TENSOR = ("tensor_0", "tensor_1")
SEQ_TENSOR = ("seq_0", "seq_1", "tensor_0", "tensor_1")
EVERYONE = ("tensor_1", "tensor_0", "seq_0", "seq_1")

epsilon = 1e-05
logit_gain = 2.0
lowest = -1e30
f32, bf16 = jnp.float32, jnp.bfloat16
VMEM = pl.BlockSpec(memory_space=pltpu.VMEM)
MIB = 1024 * 1024
PICK_GRANT = 61 * MIB
STAGE_GRANT = 49 * MIB + MIB // 2
ATTEND_GRANT = 203 * MIB // 4
HEAD_GRANT = 201 * MIB // 4
W_STAGED = 22
STAGED = 23
SMEM = pl.BlockSpec(memory_space=pltpu.SMEM)
HBM = pl.BlockSpec(memory_space=pltpu.HBM)


def exchange(copies, axis):
    return lax.all_to_all(copies, axis, split_axis=0, concat_axis=0, tiled=True)


def row_of(width=HD):
    return lax.broadcasted_iota(jnp.int32, (TILE, width), 0)


def lane_of(width=HD):
    return lax.broadcasted_iota(jnp.int32, (TILE, width), 1)


def as_line(column):
    return jnp.sum(jnp.where(row_of() == lane_of(), column, 0.0), 0, keepdims=True)


def as_column(line):
    return jnp.sum(jnp.where(row_of() == lane_of(), line, 0.0), 1, keepdims=True)


def pick_kernel(place, ids, table, out, groups, sems):
    streams = ids.shape[1]
    vocab_rows = table.shape[0]
    within, copies = [], []
    for row in range(2 * streams):
        local = ids[row // streams, row % streams] - place[0] * vocab_rows
        inside = (local >= 0) & (local < vocab_rows)
        local = jnp.clip(local, 0, vocab_rows - 1)
        offset = lax.rem(local, TILE)
        start = pl.multiple_of(local - offset, TILE)
        copy = pltpu.make_async_copy(table.at[pl.ds(start, TILE)], groups.at[row], sems.at[row])
        copy.start()
        copies.append(copy)
        within.append(jnp.where(inside, offset, TILE))
    for copy in copies:
        copy.wait()
    total = jnp.zeros((TILE, HD), f32)
    for row in range(2 * streams):
        block = groups[row].astype(f32)
        found = jnp.sum(jnp.where(row_of() == within[row], block, 0.0), 0, keepdims=True)
        total = jnp.where(row_of() == row, found, total)
    picked = total.astype(bf16)
    for peer in range(out.shape[0]):
        out[peer] = picked


def stage_kernel(after, source, out, sems):
    del after
    lead = (slice(None),) * (len(source.shape) - 2)
    chunks = sems.shape[0]
    tall = out.shape[-2] // chunks
    copies = []
    for k in range(chunks):
        part = (*lead, pl.ds(k * tall, tall))
        copies.append(pltpu.make_async_copy(source.at[part], out.at[part], sems.at[k]))
        copies[-1].start()
    for copy in copies:
        copy.wait()


def staged(after, source, rows):
    shape = (*source.shape[:-2], rows, source.shape[-1])
    return pl.pallas_call(
        stage_kernel,
        out_shape=jax.ShapeDtypeStruct(shape, source.dtype),
        in_specs=[HBM, HBM],
        out_specs=VMEM,
        scratch_shapes=[pltpu.SemaphoreType.DMA((4,))],
        compiler_params=pltpu.CompilerParams(vmem_limit_bytes=STAGE_GRANT),
        cost_estimate=pl.CostEstimate(
            flops=0, bytes_accessed=4 * math.prod(shape), transcendentals=0
        ),
        name="stage",
    )(after, source)


def attend_kernel(
    place,
    lengths,
    gathered,
    gain,
    cosine,
    sine,
    w_start,
    all_w_qkv,
    all_keys,
    all_values,
    out,
    new_kv,
    w_rest,
    keys,
    values,
    sems,
):
    streams, slots, _ = keys.shape
    first = w_start.shape[1]
    weight_copy = pltpu.make_async_copy(
        all_w_qkv.at[:, pl.ds(first, w_rest.shape[1])], w_rest, sems.at[0]
    )
    key_copy = pltpu.make_async_copy(all_keys, keys, sems.at[1])
    value_copy = pltpu.make_async_copy(all_values, values, sems.at[2])
    for copy in (weight_copy, key_copy, value_copy):
        copy.start()
    blocks = gathered.shape[0]
    width = blocks * HD
    seq = place[0]
    squares = jnp.zeros((TILE, HD), f32)
    for k in range(blocks):
        part = gathered[k].astype(f32)
        squares = squares + part * part
    scale = lax.rsqrt(jnp.sum(squares, 1, keepdims=True) / width + epsilon)
    normed = [
        (gathered[k].astype(f32) * scale * gain[k : k + 1]).astype(bf16) for k in range(blocks)
    ]
    begin = jnp.concatenate(normed[: first // HD], 1)
    rest = jnp.concatenate(normed[first // HD :], 1)
    query, key, value = (
        jnp.dot(begin, w_start[c], preferred_element_type=f32) for c in range(3)
    )
    weight_copy.wait()
    query, key, value = (
        total + jnp.dot(rest, w_rest[c], preferred_element_type=f32)
        for c, total in enumerate((query, key, value))
    )

    def rotated(part):
        return (part * cosine[...] + pltpu.roll(part, HD // 2, 1) * sine[...]).astype(bf16)

    query, key, value = rotated(query), rotated(key), value.astype(bf16)
    new_kv[0] = key
    new_kv[1] = value

    inverse = HD ** (-0.5)
    over_lanes = (((1,), (1,)), ((), ()))
    rows = row_of(slots)
    scores = jnp.zeros((TILE, slots), f32)
    length = jnp.zeros((TILE, 1), jnp.int32)
    first_lane = row_of(1)
    key_copy.wait()
    for b in range(streams):
        mine = (rows == b) | (rows == streams + b)
        some = lax.dot_general(query, keys[b], over_lanes, preferred_element_type=f32)
        scores = jnp.where(mine, some, scores)
        length = jnp.where(
            (first_lane == b) | (first_lane == streams + b), lengths[b], length
        )
    visible = lane_of(slots) + seq * slots < length
    scores = jnp.where(visible, scores * inverse, lowest)

    row, lane = row_of(TILE), lane_of(TILE)
    step, lane_step = (row >= streams).astype(jnp.int32), (lane >= streams).astype(jnp.int32)
    allowed = (row - step * streams == lane - lane_step * streams) & (lane_step <= step)
    allowed = allowed & (row < 2 * streams) & (lane < 2 * streams) & (seq == 0)
    fresh = lax.dot_general(query, key, over_lanes, preferred_element_type=f32)
    fresh = jnp.where(allowed, fresh * inverse, lowest)

    highest = jnp.maximum(jnp.max(scores, 1, keepdims=True), jnp.max(fresh, 1, keepdims=True))
    weights = jnp.where(visible, jnp.exp(scores - highest), 0.0)
    fresh_weights = jnp.where(allowed, jnp.exp(fresh - highest), 0.0)
    total = jnp.sum(weights, 1, keepdims=True) + jnp.sum(fresh_weights, 1, keepdims=True)
    mixed = jnp.dot(fresh_weights.astype(bf16), value, preferred_element_type=f32)
    value_copy.wait()
    for b in range(streams):
        mine = (rows == b) | (rows == streams + b)
        share = jnp.where(mine, weights, 0.0).astype(bf16)
        mixed = mixed + jnp.dot(share, values[b], preferred_element_type=f32)
    sent = jnp.where(row_of() == TILE - 2, as_line(highest), mixed)
    sent = jnp.where(row_of() == TILE - 1, as_line(total), sent)
    for peer in range(out.shape[0]):
        out[peer] = sent


def merge_kernel(rows, parts, w_out, out):
    count = parts.shape[0]
    peaks = [as_column(parts[k, TILE - 2 : TILE - 1, :]) for k in range(count)]
    highest = functools.reduce(jnp.maximum, peaks)
    numerator = jnp.zeros((TILE, HD), f32)
    denominator = jnp.zeros((TILE, 1), f32)
    for k in range(count):
        scale = jnp.exp(peaks[k] - highest)
        numerator = numerator + parts[k] * scale
        denominator = denominator + as_column(parts[k, TILE - 1 : TILE, :]) * scale
    real = row_of() < rows
    attended = jnp.where(real, numerator / jnp.where(real, denominator, 1.0), 0.0).astype(bf16)
    per = 8
    for group in range(out.shape[0] // per):
        some = jnp.dot(
            attended, w_out[:, group * per * HD : (group + 1) * per * HD], preferred_element_type=f32
        ).astype(bf16)
        for k in range(per):
            out[group * per + k] = some[:, k * HD : (k + 1) * HD]


def head_kernel(parts, embedded, gain, staged, whole_table, hidden_out, out, table, sem):
    peers, _, share = out.shape
    first = staged.shape[0] // share
    rest = pltpu.make_async_copy(
        whole_table.at[pl.ds(first * share, table.shape[0])], table, sem
    )
    rest.start()
    mixed = jnp.zeros((TILE, HD), f32)
    for k in range(parts.shape[0]):
        mixed = mixed + parts[k].astype(f32)
    hidden = (embedded[...].astype(f32) + mixed).astype(bf16)
    hidden_out[...] = hidden
    wide = hidden.astype(f32)
    squares = as_line(jnp.sum(wide * wide, 1, keepdims=True))
    high = squares.astype(bf16).astype(f32)
    middle = (squares - high).astype(bf16).astype(f32)
    low = squares - high - middle
    line = jnp.concatenate([high, middle, low, jnp.zeros((1, share - 3 * HD), f32)], 1)
    gated = (wide * gain[...]).astype(bf16)
    spare = row_of(share) == TILE - 1
    for k in range(peers):
        source, at = (staged, k) if k < first else (table, k - first)
        if k == first:
            rest.wait()
        some = lax.dot_general(
            gated,
            source[at * share : (at + 1) * share, :],
            (((1,), (1,)), ((), ())),
            preferred_element_type=f32,
        )
        out[k] = jnp.where(spare, line, some).astype(bf16)


def share_kernel(model_width, parts, shares_out, lines_out):
    total = parts[0].astype(f32)
    for k in range(1, parts.shape[0]):
        total = total + parts[k].astype(f32)
    line = total[TILE - 1 :, :]
    squares = as_column(line[:, :HD] + line[:, HD : 2 * HD] + line[:, 2 * HD : 3 * HD])
    factor = lax.rsqrt(squares / model_width + epsilon) * (logit_gain / math.sqrt(model_width))
    shares = total * factor
    shares_out[...] = shares
    highest = jnp.max(shares, 1, keepdims=True)
    summed = jnp.sum(jnp.exp(shares - highest), 1, keepdims=True)
    sent = as_line(highest) + pltpu.roll(as_line(summed), HD // 2, 1)
    lines_out[...] = jnp.broadcast_to(sent.reshape(1, 1, HD), lines_out.shape)


def finish_kernel(shares, lines, out):
    every = lines[...]
    highest = jnp.max(jnp.max(every, 0), 0, keepdims=True)
    scaled = jnp.exp(every - highest.reshape(1, 1, HD)) * pltpu.roll(every, HD // 2, 2)
    summed = jnp.sum(jnp.sum(scaled, 0), 0, keepdims=True)
    lane = lax.broadcasted_iota(jnp.int32, summed.shape, 1)
    summed = jnp.where(lane < TILE, summed, 1.0)
    total = as_column(highest + jnp.log(summed))
    logprobs = shares[...] - total
    streams = out.shape[0]
    for b in range(streams):
        out[b, 0:1, :] = logprobs[b : b + 1, :]
        out[b, 1:2, :] = logprobs[streams + b : streams + b + 1, :]


def body(
    token_ids,
    cache_lengths,
    embed_table,
    attn_gain,
    final_gain,
    w_qkv,
    w_out,
    cache_keys,
    cache_values,
):
    streams = token_ids.shape[1]
    rows = 2 * streams
    vocab_rows, local_width = embed_table.shape
    model_width = attn_gain.shape[0]
    seqs, peers = lax.axis_size(SEQ), lax.axis_size(TENSOR)
    tensor_index = lax.axis_index(TENSOR)
    place = lax.axis_index(SEQ).astype(jnp.int32).reshape(1)
    params = pltpu.CompilerParams(vmem_limit_bytes=16 * 1024 * 1024)
    shape = jax.ShapeDtypeStruct

    picked = pl.pallas_call(
        pick_kernel,
        out_shape=shape((seqs, TILE, HD), bf16),
        in_specs=[SMEM, SMEM, HBM],
        out_specs=VMEM,
        scratch_shapes=[
            pltpu.VMEM((rows, TILE, HD), bf16),
            pltpu.SemaphoreType.DMA((rows,)),
        ],
        compiler_params=pltpu.CompilerParams(vmem_limit_bytes=PICK_GRANT),
        cost_estimate=pl.CostEstimate(flops=0, bytes_accessed=2**17, transcendentals=0),
        name="pick",
    )(place, token_ids, embed_table)
    embedded = jnp.sum(exchange(picked, SEQ).astype(f32), 0).astype(bf16)
    gathered = exchange(jnp.broadcast_to(embedded, (peers, TILE, HD)), TENSOR)

    positions = (cache_lengths[None, :] + jnp.arange(2, dtype=jnp.int32)[:, None]).reshape(rows)
    half = HD // 2
    frequency = 10000.0 ** (-(jnp.arange(half, dtype=f32) * 2.0 / HD))
    angles = positions.astype(f32)[:, None] * frequency
    cosine, sine = jnp.cos(angles), jnp.sin(angles)
    padding = ((0, TILE - rows), (0, 0))
    cosine = jnp.pad(jnp.concatenate([cosine, cosine], 1), padding)
    sine = jnp.pad(jnp.concatenate([-sine, sine], 1), padding)

    w_qkv = jnp.moveaxis(w_qkv, 1, 0)
    w_rows = model_width * W_STAGED // 32
    parts, new_kv = pl.pallas_call(
        attend_kernel,
        out_shape=(shape((seqs, TILE, HD), f32), shape((2, TILE, HD), bf16)),
        in_specs=[SMEM, SMEM] + [VMEM] * 5 + [HBM] * 3,
        out_specs=(VMEM, VMEM),
        scratch_shapes=[
            pltpu.VMEM((3, model_width - w_rows, HD), bf16),
            pltpu.VMEM(cache_keys.shape, bf16),
            pltpu.VMEM(cache_values.shape, bf16),
            pltpu.SemaphoreType.DMA((3,)),
        ],
        compiler_params=pltpu.CompilerParams(vmem_limit_bytes=ATTEND_GRANT),
        name="attend",
    )(
        place,
        cache_lengths,
        gathered,
        attn_gain.reshape(peers, HD),
        cosine,
        sine,
        staged(embedded, w_qkv, w_rows),
        w_qkv,
        cache_keys,
        cache_values,
    )
    mixed = pl.pallas_call(
        functools.partial(merge_kernel, rows),
        out_shape=shape((peers, TILE, HD), bf16),
        in_specs=[VMEM, VMEM],
        out_specs=VMEM,
        compiler_params=params,
        name="merge",
    )(exchange(parts, SEQ), w_out)
    share_width = vocab_rows // peers
    staged_rows = STAGED * peers // 32 * share_width
    table_start = staged(mixed, embed_table, staged_rows)
    hidden, sent = pl.pallas_call(
        head_kernel,
        out_shape=(shape((TILE, HD), bf16), shape((peers, TILE, share_width), bf16)),
        in_specs=[VMEM] * 4 + [HBM],
        out_specs=(VMEM, VMEM),
        scratch_shapes=[
            pltpu.VMEM((vocab_rows - staged_rows, HD), bf16),
            pltpu.SemaphoreType.DMA,
        ],
        compiler_params=pltpu.CompilerParams(vmem_limit_bytes=HEAD_GRANT),
        name="head",
    )(
        exchange(mixed, TENSOR),
        embedded,
        lax.dynamic_slice_in_dim(final_gain, tensor_index * HD, HD).reshape(1, HD),
        table_start,
        embed_table,
    )
    everyone = seqs * peers
    shares, lines = pl.pallas_call(
        functools.partial(share_kernel, model_width),
        out_shape=(shape((TILE, share_width), f32), shape((everyone // 8, 8, HD), f32)),
        in_specs=[VMEM],
        out_specs=(VMEM, VMEM),
        compiler_params=params,
        name="share",
    )(exchange(sent, TENSOR))
    logprobs = pl.pallas_call(
        finish_kernel,
        out_shape=shape((streams, 2, share_width), f32),
        in_specs=[VMEM, VMEM],
        out_specs=VMEM,
        compiler_params=params,
        name="finish",
    )(shares, exchange(lines.reshape(everyone, 1, HD), EVERYONE).reshape(lines.shape))
    return (
        hidden[:rows].reshape(2, streams, local_width),
        new_kv[:, :rows].reshape(2, 2, streams, local_width),
        jnp.swapaxes(logprobs, 0, 1),
    )


def solution(mesh):
    split = Mesh(mesh.devices.reshape(4, 2, 4, 8), ("seq_0", "seq_1", "tensor_0", "tensor_1"))
    placed = (
        P(),
        P(),
        P(SEQ, TENSOR),
        P(),
        P(),
        P(None, None, TENSOR),
        P(TENSOR, None),
        P(None, SEQ, TENSOR),
        P(None, SEQ, TENSOR),
    )
    return jax.shard_map(
        body,
        mesh=split,
        in_specs=placed,
        out_specs=(P(None, None, TENSOR), P(None, None, None, TENSOR), P(None, None, SEQ_TENSOR)),
        check_vma=False,
    )
```

```python
import functools
import math

import jax
import jax.numpy as jnp
from jax import lax
from jax.experimental import pallas as pl
from jax.experimental.pallas import tpu as pltpu
from jax.sharding import Mesh
from jax.sharding import PartitionSpec as P

HD = 128
TILE = 16
SEQ = ("seq_0", "seq_1")
TENSOR = ("tensor_0", "tensor_1")
SEQ_TENSOR = ("seq_0", "seq_1", "tensor_0", "tensor_1")
EVERYONE = ("tensor_1", "tensor_0", "seq_0", "seq_1")

epsilon = 1e-05
logit_gain = 2.0
lowest = -1e30
f32, bf16 = jnp.float32, jnp.bfloat16
VMEM = pl.BlockSpec(memory_space=pltpu.VMEM)
MIB = 1024 * 1024
PICK_GRANT = 61 * MIB
STAGE_GRANT = 49 * MIB + MIB // 2
ATTEND_GRANT = 203 * MIB // 4
HEAD_GRANT = 201 * MIB // 4
W_STAGED = 22
STAGED = 23
SMEM = pl.BlockSpec(memory_space=pltpu.SMEM)
HBM = pl.BlockSpec(memory_space=pltpu.HBM)


def exchange(copies, axis):
    return lax.all_to_all(copies, axis, split_axis=0, concat_axis=0, tiled=True)


def row_of(width=HD):
    return lax.broadcasted_iota(jnp.int32, (TILE, width), 0)


def lane_of(width=HD):
    return lax.broadcasted_iota(jnp.int32, (TILE, width), 1)


def as_line(column):
    return jnp.sum(jnp.where(row_of() == lane_of(), column, 0.0), 0, keepdims=True)


def as_column(line):
    return jnp.sum(jnp.where(row_of() == lane_of(), line, 0.0), 1, keepdims=True)


def thirds(value):
    high = value.astype(bf16).astype(f32)
    middle = (value - high).astype(bf16).astype(f32)
    return high, middle, value - high - middle


def packed(column):
    high, middle, low = thirds(as_line(column))
    return high + pltpu.roll(middle, TILE, 1) + pltpu.roll(low, 2 * TILE, 1)


def unpacked(line):
    line = line + pltpu.roll(line, HD - TILE, 1) + pltpu.roll(line, HD - 2 * TILE, 1)
    return as_column(line)


def pick_kernel(place, ids, table, out, groups, sems):
    streams = ids.shape[1]
    vocab_rows = table.shape[0]
    within, copies = [], []
    for row in range(2 * streams):
        local = ids[row // streams, row % streams] - place[0] * vocab_rows
        inside = (local >= 0) & (local < vocab_rows)
        local = jnp.clip(local, 0, vocab_rows - 1)
        offset = local & (TILE - 1)
        start = pl.multiple_of(local - offset, TILE)
        copy = pltpu.make_async_copy(
            table.at[pl.ds(start, TILE)], groups.at[pl.ds(row * TILE, TILE)], sems.at[row]
        )
        copy.start()
        copies.append(copy)
        within.append(jnp.where(inside, row * TILE + offset, -1))
    for copy in copies:
        copy.wait()
    row_at = row_of(groups.shape[0])
    target = jnp.full(row_at.shape, -1, jnp.int32)
    for row, at in enumerate(within):
        target = jnp.where(row_at == row, at, target)
    chosen = (target == lane_of(groups.shape[0])).astype(f32).astype(bf16)
    total = jnp.dot(chosen, groups[...], preferred_element_type=f32)
    picked = total.astype(bf16)
    for peer in range(out.shape[0]):
        out[peer] = picked


def stage_kernel(after, source, out, sems):
    del after
    lead = (slice(None),) * (len(source.shape) - 2)
    chunks = sems.shape[0]
    tall = out.shape[-2] // chunks
    copies = []
    for k in range(chunks):
        part = (*lead, pl.ds(k * tall, tall))
        copies.append(pltpu.make_async_copy(source.at[part], out.at[part], sems.at[k]))
        copies[-1].start()
    for copy in copies:
        copy.wait()


def staged(after, source, rows):
    shape = (*source.shape[:-2], rows, source.shape[-1])
    return pl.pallas_call(
        stage_kernel,
        out_shape=jax.ShapeDtypeStruct(shape, source.dtype),
        in_specs=[HBM, HBM],
        out_specs=VMEM,
        scratch_shapes=[pltpu.SemaphoreType.DMA((4,))],
        compiler_params=pltpu.CompilerParams(vmem_limit_bytes=STAGE_GRANT),
        cost_estimate=pl.CostEstimate(
            flops=0, bytes_accessed=4 * math.prod(shape), transcendentals=0
        ),
        name="stage",
    )(after, source)


def attend_kernel(
    place,
    lengths,
    gathered,
    gain,
    cosine,
    sine,
    w_start,
    all_w_qkv,
    all_keys,
    all_values,
    out,
    new_kv,
    w_rest,
    keys,
    values,
    sems,
):
    streams, slots, _ = keys.shape
    first = w_start.shape[1]
    weight_copy = pltpu.make_async_copy(
        all_w_qkv.at[:, pl.ds(first, w_rest.shape[1])], w_rest, sems.at[0]
    )
    key_copy = pltpu.make_async_copy(all_keys, keys, sems.at[1])
    value_copy = pltpu.make_async_copy(all_values, values, sems.at[2])
    for copy in (weight_copy, key_copy, value_copy):
        copy.start()
    blocks = gathered.shape[0]
    width = blocks * HD
    seq = place[0]
    squares = jnp.zeros((TILE, HD), f32)
    for k in range(blocks):
        part = gathered[k].astype(f32)
        squares = squares + part * part
    scale = lax.rsqrt(jnp.sum(squares, 1, keepdims=True) / width + epsilon)
    normed = [
        (gathered[k].astype(f32) * scale * gain[k : k + 1]).astype(bf16) for k in range(blocks)
    ]
    begin = jnp.concatenate(normed[: first // HD], 1)
    rest = jnp.concatenate(normed[first // HD :], 1)
    query, key, value = (
        jnp.dot(begin, w_start[c], preferred_element_type=f32) for c in range(3)
    )
    weight_copy.wait()
    query, key, value = (
        total + jnp.dot(rest, w_rest[c], preferred_element_type=f32)
        for c, total in enumerate((query, key, value))
    )

    def rotated(part):
        return (part * cosine[...] + pltpu.roll(part, HD // 2, 1) * sine[...]).astype(bf16)

    query, key, value = rotated(query), rotated(key), value.astype(bf16)
    new_kv[0] = key
    new_kv[1] = value

    inverse = HD ** (-0.5)
    over_lanes = (((1,), (1,)), ((), ()))
    rows = row_of(slots)
    scores = jnp.zeros((TILE, slots), f32)
    length = jnp.zeros((TILE, 1), jnp.int32)
    first_lane = row_of(1)
    key_copy.wait()
    for b in range(streams):
        mine = (rows == b) | (rows == streams + b)
        some = lax.dot_general(query, keys[b], over_lanes, preferred_element_type=f32)
        scores = jnp.where(mine, some, scores)
        length = jnp.where(
            (first_lane == b) | (first_lane == streams + b), lengths[b], length
        )
    visible = lane_of(slots) + seq * slots < length
    scores = jnp.where(visible, scores * inverse, lowest)

    row, lane = row_of(TILE), lane_of(TILE)
    step, lane_step = (row >= streams).astype(jnp.int32), (lane >= streams).astype(jnp.int32)
    allowed = (row - step * streams == lane - lane_step * streams) & (lane_step <= step)
    allowed = allowed & (row < 2 * streams) & (lane < 2 * streams) & (seq == 0)
    fresh = lax.dot_general(query, key, over_lanes, preferred_element_type=f32)
    fresh = jnp.where(allowed, fresh * inverse, lowest)

    highest = jnp.maximum(jnp.max(scores, 1, keepdims=True), jnp.max(fresh, 1, keepdims=True))
    weights = jnp.where(visible, jnp.exp(scores - highest), 0.0)
    fresh_weights = jnp.where(allowed, jnp.exp(fresh - highest), 0.0)
    total = jnp.sum(weights, 1, keepdims=True) + jnp.sum(fresh_weights, 1, keepdims=True)
    mixed = jnp.dot(fresh_weights.astype(bf16), value, preferred_element_type=f32)
    value_copy.wait()
    for b in range(streams):
        mine = (rows == b) | (rows == streams + b)
        share = jnp.where(mine, weights, 0.0).astype(bf16)
        mixed = mixed + jnp.dot(share, values[b], preferred_element_type=f32)
    sent = jnp.where(row_of() == TILE - 2, packed(highest), mixed)
    sent = jnp.where(row_of() == TILE - 1, packed(total), sent).astype(bf16)
    for peer in range(out.shape[0]):
        out[peer] = sent


def merge_kernel(rows, parts, w_out, out):
    blocks = [parts[k].astype(f32) for k in range(parts.shape[0])]
    peaks = [unpacked(block[TILE - 2 : TILE - 1, :]) for block in blocks]
    highest = functools.reduce(jnp.maximum, peaks)
    numerator = jnp.zeros((TILE, HD), f32)
    denominator = jnp.zeros((TILE, 1), f32)
    for block, peak in zip(blocks, peaks):
        scale = jnp.exp(peak - highest)
        numerator = numerator + block * scale
        denominator = denominator + unpacked(block[TILE - 1 : TILE, :]) * scale
    real = row_of() < rows
    attended = jnp.where(real, numerator / jnp.where(real, denominator, 1.0), 0.0).astype(bf16)
    per = 8
    for group in range(out.shape[0] // per):
        some = jnp.dot(
            attended, w_out[:, group * per * HD : (group + 1) * per * HD], preferred_element_type=f32
        ).astype(bf16)
        for k in range(per):
            out[group * per + k] = some[:, k * HD : (k + 1) * HD]


def head_kernel(parts, embedded, gain, staged, whole_table, hidden_out, out, table, sem):
    peers, _, share = out.shape
    first = staged.shape[0] // share
    rest = pltpu.make_async_copy(
        whole_table.at[pl.ds(first * share, table.shape[0])], table, sem
    )
    rest.start()
    mixed = jnp.zeros((TILE, HD), f32)
    for k in range(parts.shape[0]):
        mixed = mixed + parts[k].astype(f32)
    hidden = (embedded[...].astype(f32) + mixed).astype(bf16)
    hidden_out[...] = hidden
    wide = hidden.astype(f32)
    squares = as_line(jnp.sum(wide * wide, 1, keepdims=True))
    line = jnp.concatenate([*thirds(squares), jnp.zeros((1, share - 3 * HD), f32)], 1)
    gated = (wide * gain[...]).astype(bf16)
    spare = row_of(share) == TILE - 1
    for k in range(peers):
        source, at = (staged, k) if k < first else (table, k - first)
        if k == first:
            rest.wait()
        some = lax.dot_general(
            gated,
            source[at * share : (at + 1) * share, :],
            (((1,), (1,)), ((), ())),
            preferred_element_type=f32,
        )
        out[k] = jnp.where(spare, line, some).astype(bf16)


def share_kernel(model_width, parts, shares_out, lines_out):
    total = parts[0].astype(f32)
    for k in range(1, parts.shape[0]):
        total = total + parts[k].astype(f32)
    line = total[TILE - 1 :, :]
    squares = as_column(line[:, :HD] + line[:, HD : 2 * HD] + line[:, 2 * HD : 3 * HD])
    factor = lax.rsqrt(squares / model_width + epsilon) * (logit_gain / math.sqrt(model_width))
    shares = total * factor
    shares_out[...] = shares
    highest = jnp.max(shares, 1, keepdims=True)
    summed = jnp.sum(jnp.exp(shares - highest), 1, keepdims=True)
    sent = as_line(highest) + pltpu.roll(as_line(summed), HD // 2, 1)
    lines_out[...] = jnp.broadcast_to(sent.reshape(1, 1, HD), lines_out.shape)


def finish_kernel(shares, lines, out):
    every = lines[...]
    highest = jnp.max(jnp.max(every, 0), 0, keepdims=True)
    scaled = jnp.exp(every - highest.reshape(1, 1, HD)) * pltpu.roll(every, HD // 2, 2)
    summed = jnp.sum(jnp.sum(scaled, 0), 0, keepdims=True)
    lane = lax.broadcasted_iota(jnp.int32, summed.shape, 1)
    summed = jnp.where(lane < TILE, summed, 1.0)
    total = as_column(highest + jnp.log(summed))
    logprobs = shares[...] - total
    streams = out.shape[0]
    for b in range(streams):
        out[b, 0:1, :] = logprobs[b : b + 1, :]
        out[b, 1:2, :] = logprobs[streams + b : streams + b + 1, :]


def body(
    token_ids,
    cache_lengths,
    embed_table,
    attn_gain,
    final_gain,
    w_qkv,
    w_out,
    cache_keys,
    cache_values,
):
    streams = token_ids.shape[1]
    rows = 2 * streams
    vocab_rows, local_width = embed_table.shape
    model_width = attn_gain.shape[0]
    seqs, peers = lax.axis_size(SEQ), lax.axis_size(TENSOR)
    tensor_index = lax.axis_index(TENSOR)
    place = lax.axis_index(SEQ).astype(jnp.int32).reshape(1)
    params = pltpu.CompilerParams(vmem_limit_bytes=16 * 1024 * 1024)
    shape = jax.ShapeDtypeStruct

    picked = pl.pallas_call(
        pick_kernel,
        out_shape=shape((seqs, TILE, HD), bf16),
        in_specs=[SMEM, SMEM, HBM],
        out_specs=VMEM,
        scratch_shapes=[
            pltpu.VMEM((rows * TILE, HD), bf16),
            pltpu.SemaphoreType.DMA((rows,)),
        ],
        compiler_params=pltpu.CompilerParams(vmem_limit_bytes=PICK_GRANT),
        cost_estimate=pl.CostEstimate(flops=0, bytes_accessed=2**17, transcendentals=0),
        name="pick",
    )(place, token_ids, embed_table)
    embedded = jnp.sum(exchange(picked, SEQ).astype(f32), 0).astype(bf16)
    gathered = exchange(jnp.broadcast_to(embedded, (peers, TILE, HD)), TENSOR)

    positions = (cache_lengths[None, :] + jnp.arange(2, dtype=jnp.int32)[:, None]).reshape(rows)
    half = HD // 2
    frequency = 10000.0 ** (-(jnp.arange(half, dtype=f32) * 2.0 / HD))
    angles = positions.astype(f32)[:, None] * frequency
    cosine, sine = jnp.cos(angles), jnp.sin(angles)
    padding = ((0, TILE - rows), (0, 0))
    cosine = jnp.pad(jnp.concatenate([cosine, cosine], 1), padding)
    sine = jnp.pad(jnp.concatenate([-sine, sine], 1), padding)

    w_qkv = jnp.moveaxis(w_qkv, 1, 0)
    w_rows = model_width * W_STAGED // 32
    parts, new_kv = pl.pallas_call(
        attend_kernel,
        out_shape=(shape((seqs, TILE, HD), bf16), shape((2, TILE, HD), bf16)),
        in_specs=[SMEM, SMEM] + [VMEM] * 5 + [HBM] * 3,
        out_specs=(VMEM, VMEM),
        scratch_shapes=[
            pltpu.VMEM((3, model_width - w_rows, HD), bf16),
            pltpu.VMEM(cache_keys.shape, bf16),
            pltpu.VMEM(cache_values.shape, bf16),
            pltpu.SemaphoreType.DMA((3,)),
        ],
        compiler_params=pltpu.CompilerParams(vmem_limit_bytes=ATTEND_GRANT),
        name="attend",
    )(
        place,
        cache_lengths,
        gathered,
        attn_gain.reshape(peers, HD),
        cosine,
        sine,
        staged(embedded, w_qkv, w_rows),
        w_qkv,
        cache_keys,
        cache_values,
    )
    mixed = pl.pallas_call(
        functools.partial(merge_kernel, rows),
        out_shape=shape((peers, TILE, HD), bf16),
        in_specs=[VMEM, VMEM],
        out_specs=VMEM,
        compiler_params=params,
        name="merge",
    )(exchange(parts, SEQ), w_out)
    share_width = vocab_rows // peers
    staged_rows = STAGED * peers // 32 * share_width
    table_start = staged(mixed, embed_table, staged_rows)
    hidden, sent = pl.pallas_call(
        head_kernel,
        out_shape=(shape((TILE, HD), bf16), shape((peers, TILE, share_width), bf16)),
        in_specs=[VMEM] * 4 + [HBM],
        out_specs=(VMEM, VMEM),
        scratch_shapes=[
            pltpu.VMEM((vocab_rows - staged_rows, HD), bf16),
            pltpu.SemaphoreType.DMA,
        ],
        compiler_params=pltpu.CompilerParams(vmem_limit_bytes=HEAD_GRANT),
        name="head",
    )(
        exchange(mixed, TENSOR),
        embedded,
        lax.dynamic_slice_in_dim(final_gain, tensor_index * HD, HD).reshape(1, HD),
        table_start,
        embed_table,
    )
    everyone = seqs * peers
    shares, lines = pl.pallas_call(
        functools.partial(share_kernel, model_width),
        out_shape=(shape((TILE, share_width), f32), shape((everyone // 8, 8, HD), f32)),
        in_specs=[VMEM],
        out_specs=(VMEM, VMEM),
        compiler_params=params,
        name="share",
    )(exchange(sent, TENSOR))
    logprobs = pl.pallas_call(
        finish_kernel,
        out_shape=shape((streams, 2, share_width), f32),
        in_specs=[VMEM, VMEM],
        out_specs=VMEM,
        compiler_params=params,
        name="finish",
    )(shares, exchange(lines.reshape(everyone, 1, HD), EVERYONE).reshape(lines.shape))
    return (
        hidden[:rows].reshape(2, streams, local_width),
        new_kv[:, :rows].reshape(2, 2, streams, local_width),
        jnp.swapaxes(logprobs, 0, 1),
    )


def solution(mesh):
    split = Mesh(mesh.devices.reshape(4, 2, 4, 8), ("seq_0", "seq_1", "tensor_0", "tensor_1"))
    placed = (
        P(),
        P(),
        P(SEQ, TENSOR),
        P(),
        P(),
        P(None, None, TENSOR),
        P(TENSOR, None),
        P(None, SEQ, TENSOR),
        P(None, SEQ, TENSOR),
    )
    return jax.shard_map(
        body,
        mesh=split,
        in_specs=placed,
        out_specs=(P(None, None, TENSOR), P(None, None, None, TENSOR), P(None, None, SEQ_TENSOR)),
        check_vma=False,
    )
```

```python
import functools
import math

import jax
import jax.numpy as jnp
from jax import lax
from jax.experimental import pallas as pl
from jax.experimental.pallas import tpu as pltpu
from jax.sharding import Mesh
from jax.sharding import PartitionSpec as P

HD = 128
TILE = 16
SEQ = ("seq_0", "seq_1")
TENSOR = ("tensor_0", "tensor_1")
SEQ_TENSOR = ("seq_0", "seq_1", "tensor_0", "tensor_1")
EVERYONE = ("tensor_1", "tensor_0", "seq_0", "seq_1")

epsilon = 1e-05
logit_gain = 2.0
lowest = -1e30
f32, bf16 = jnp.float32, jnp.bfloat16
VMEM = pl.BlockSpec(memory_space=pltpu.VMEM)
MIB = 1024 * 1024
PICK_GRANT = 61 * MIB
STAGE_GRANT = 49 * MIB + MIB // 2
ATTEND_GRANT = 203 * MIB // 4
HEAD_GRANT = 201 * MIB // 4
W_STAGED = 22
STAGED = 23
SMEM = pl.BlockSpec(memory_space=pltpu.SMEM)
HBM = pl.BlockSpec(memory_space=pltpu.HBM)


def slot_of(block):
    planes, depth = lax.axis_size(TENSOR[0]), lax.axis_size(TENSOR[1])
    return block % depth * planes + block // depth


def exchange(copies, axis):
    return lax.all_to_all(copies, axis, split_axis=0, concat_axis=0, tiled=True)


def row_of(width=HD):
    return lax.broadcasted_iota(jnp.int32, (TILE, width), 0)


def lane_of(width=HD):
    return lax.broadcasted_iota(jnp.int32, (TILE, width), 1)


def as_line(column):
    return jnp.sum(jnp.where(row_of() == lane_of(), column, 0.0), 0, keepdims=True)


def as_column(line):
    return jnp.sum(jnp.where(row_of() == lane_of(), line, 0.0), 1, keepdims=True)


def pick_kernel(place, ids, table, out, groups, sems):
    streams = ids.shape[1]
    vocab_rows = table.shape[0]
    within, copies = [], []
    for row in range(2 * streams):
        local = ids[row // streams, row % streams] - place[0] * vocab_rows
        inside = (local >= 0) & (local < vocab_rows)
        local = jnp.clip(local, 0, vocab_rows - 1)
        offset = lax.rem(local, TILE)
        start = pl.multiple_of(local - offset, TILE)
        copy = pltpu.make_async_copy(table.at[pl.ds(start, TILE)], groups.at[row], sems.at[row])
        copy.start()
        copies.append(copy)
        within.append(jnp.where(inside, offset, TILE))
    for copy in copies:
        copy.wait()
    total = jnp.zeros((TILE, HD), f32)
    for row in range(2 * streams):
        block = groups[row].astype(f32)
        found = jnp.sum(jnp.where(row_of() == within[row], block, 0.0), 0, keepdims=True)
        total = jnp.where(row_of() == row, found, total)
    picked = total.astype(bf16)
    for peer in range(out.shape[0]):
        out[peer] = picked


def stage_kernel(after, source, out, sems):
    del after
    lead = (slice(None),) * (len(source.shape) - 2)
    chunks = sems.shape[0]
    tall = out.shape[-2] // chunks
    copies = []
    for k in range(chunks):
        part = (*lead, pl.ds(k * tall, tall))
        copies.append(pltpu.make_async_copy(source.at[part], out.at[part], sems.at[k]))
        copies[-1].start()
    for copy in copies:
        copy.wait()


def staged(after, source, rows):
    shape = (*source.shape[:-2], rows, source.shape[-1])
    return pl.pallas_call(
        stage_kernel,
        out_shape=jax.ShapeDtypeStruct(shape, source.dtype),
        in_specs=[HBM, HBM],
        out_specs=VMEM,
        scratch_shapes=[pltpu.SemaphoreType.DMA((4,))],
        compiler_params=pltpu.CompilerParams(vmem_limit_bytes=STAGE_GRANT),
        cost_estimate=pl.CostEstimate(
            flops=0, bytes_accessed=4 * math.prod(shape), transcendentals=0
        ),
        name="stage",
    )(after, source)


def attend_kernel(
    slots_at,
    place,
    lengths,
    gathered,
    gain,
    cosine,
    sine,
    w_start,
    all_w_qkv,
    all_keys,
    all_values,
    out,
    new_kv,
    w_rest,
    keys,
    values,
    sems,
):
    streams, slots, _ = keys.shape
    first = w_start.shape[1]
    weight_copy = pltpu.make_async_copy(
        all_w_qkv.at[:, pl.ds(first, w_rest.shape[1])], w_rest, sems.at[0]
    )
    key_copy = pltpu.make_async_copy(all_keys, keys, sems.at[1])
    value_copy = pltpu.make_async_copy(all_values, values, sems.at[2])
    for copy in (weight_copy, key_copy, value_copy):
        copy.start()
    blocks = gathered.shape[0]
    width = blocks * HD
    seq = place[0]
    squares = jnp.zeros((TILE, HD), f32)
    for k in range(blocks):
        part = gathered[k].astype(f32)
        squares = squares + part * part
    scale = lax.rsqrt(jnp.sum(squares, 1, keepdims=True) / width + epsilon)
    normed = [
        (gathered[slots_at[k]].astype(f32) * scale * gain[k : k + 1]).astype(bf16) for k in range(blocks)
    ]
    begin = jnp.concatenate(normed[: first // HD], 1)
    rest = jnp.concatenate(normed[first // HD :], 1)
    query, key, value = (
        jnp.dot(begin, w_start[c], preferred_element_type=f32) for c in range(3)
    )
    weight_copy.wait()
    query, key, value = (
        total + jnp.dot(rest, w_rest[c], preferred_element_type=f32)
        for c, total in enumerate((query, key, value))
    )

    def rotated(part):
        return (part * cosine[...] + pltpu.roll(part, HD // 2, 1) * sine[...]).astype(bf16)

    query, key, value = rotated(query), rotated(key), value.astype(bf16)
    new_kv[0] = key
    new_kv[1] = value

    inverse = HD ** (-0.5)
    over_lanes = (((1,), (1,)), ((), ()))
    rows = row_of(slots)
    scores = jnp.zeros((TILE, slots), f32)
    length = jnp.zeros((TILE, 1), jnp.int32)
    first_lane = row_of(1)
    key_copy.wait()
    for b in range(streams):
        mine = (rows == b) | (rows == streams + b)
        some = lax.dot_general(query, keys[b], over_lanes, preferred_element_type=f32)
        scores = jnp.where(mine, some, scores)
        length = jnp.where(
            (first_lane == b) | (first_lane == streams + b), lengths[b], length
        )
    visible = lane_of(slots) + seq * slots < length
    scores = jnp.where(visible, scores * inverse, lowest)

    row, lane = row_of(TILE), lane_of(TILE)
    step, lane_step = (row >= streams).astype(jnp.int32), (lane >= streams).astype(jnp.int32)
    allowed = (row - step * streams == lane - lane_step * streams) & (lane_step <= step)
    allowed = allowed & (row < 2 * streams) & (lane < 2 * streams) & (seq == 0)
    fresh = lax.dot_general(query, key, over_lanes, preferred_element_type=f32)
    fresh = jnp.where(allowed, fresh * inverse, lowest)

    highest = jnp.maximum(jnp.max(scores, 1, keepdims=True), jnp.max(fresh, 1, keepdims=True))
    weights = jnp.where(visible, jnp.exp(scores - highest), 0.0)
    fresh_weights = jnp.where(allowed, jnp.exp(fresh - highest), 0.0)
    total = jnp.sum(weights, 1, keepdims=True) + jnp.sum(fresh_weights, 1, keepdims=True)
    mixed = jnp.dot(fresh_weights.astype(bf16), value, preferred_element_type=f32)
    value_copy.wait()
    for b in range(streams):
        mine = (rows == b) | (rows == streams + b)
        share = jnp.where(mine, weights, 0.0).astype(bf16)
        mixed = mixed + jnp.dot(share, values[b], preferred_element_type=f32)
    sent = jnp.where(row_of() == TILE - 2, as_line(highest), mixed)
    sent = jnp.where(row_of() == TILE - 1, as_line(total), sent)
    for peer in range(out.shape[0]):
        out[peer] = sent


def merge_kernel(rows, slots_at, parts, w_out, out):
    count = parts.shape[0]
    peaks = [as_column(parts[k, TILE - 2 : TILE - 1, :]) for k in range(count)]
    highest = functools.reduce(jnp.maximum, peaks)
    numerator = jnp.zeros((TILE, HD), f32)
    denominator = jnp.zeros((TILE, 1), f32)
    for k in range(count):
        scale = jnp.exp(peaks[k] - highest)
        numerator = numerator + parts[k] * scale
        denominator = denominator + as_column(parts[k, TILE - 1 : TILE, :]) * scale
    real = row_of() < rows
    attended = jnp.where(real, numerator / jnp.where(real, denominator, 1.0), 0.0).astype(bf16)
    per = 8
    for group in range(out.shape[0] // per):
        some = jnp.dot(
            attended, w_out[:, group * per * HD : (group + 1) * per * HD], preferred_element_type=f32
        ).astype(bf16)
        for k in range(per):
            out[slots_at[group * per + k]] = some[:, k * HD : (k + 1) * HD]


def head_kernel(slots_at, parts, embedded, gain, staged, whole_table, hidden_out, out, table, sem):
    peers, _, share = out.shape
    first = staged.shape[0] // share
    rest = pltpu.make_async_copy(
        whole_table.at[pl.ds(first * share, table.shape[0])], table, sem
    )
    rest.start()
    mixed = jnp.zeros((TILE, HD), f32)
    for k in range(parts.shape[0]):
        mixed = mixed + parts[k].astype(f32)
    hidden = (embedded[...].astype(f32) + mixed).astype(bf16)
    hidden_out[...] = hidden
    wide = hidden.astype(f32)
    squares = as_line(jnp.sum(wide * wide, 1, keepdims=True))
    high = squares.astype(bf16).astype(f32)
    middle = (squares - high).astype(bf16).astype(f32)
    low = squares - high - middle
    line = jnp.concatenate([high, middle, low, jnp.zeros((1, share - 3 * HD), f32)], 1)
    gated = (wide * gain[...]).astype(bf16)
    spare = row_of(share) == TILE - 1
    for k in range(peers):
        source, at = (staged, k) if k < first else (table, k - first)
        if k == first:
            rest.wait()
        some = lax.dot_general(
            gated,
            source[at * share : (at + 1) * share, :],
            (((1,), (1,)), ((), ())),
            preferred_element_type=f32,
        )
        out[slots_at[k]] = jnp.where(spare, line, some).astype(bf16)


def share_kernel(model_width, parts, shares_out, lines_out):
    total = parts[0].astype(f32)
    for k in range(1, parts.shape[0]):
        total = total + parts[k].astype(f32)
    line = total[TILE - 1 :, :]
    squares = as_column(line[:, :HD] + line[:, HD : 2 * HD] + line[:, 2 * HD : 3 * HD])
    factor = lax.rsqrt(squares / model_width + epsilon) * (logit_gain / math.sqrt(model_width))
    shares = total * factor
    shares_out[...] = shares
    highest = jnp.max(shares, 1, keepdims=True)
    summed = jnp.sum(jnp.exp(shares - highest), 1, keepdims=True)
    sent = as_line(highest) + pltpu.roll(as_line(summed), HD // 2, 1)
    lines_out[...] = jnp.broadcast_to(sent.reshape(1, 1, HD), lines_out.shape)


def finish_kernel(shares, lines, out):
    every = lines[...]
    highest = jnp.max(jnp.max(every, 0), 0, keepdims=True)
    scaled = jnp.exp(every - highest.reshape(1, 1, HD)) * pltpu.roll(every, HD // 2, 2)
    summed = jnp.sum(jnp.sum(scaled, 0), 0, keepdims=True)
    lane = lax.broadcasted_iota(jnp.int32, summed.shape, 1)
    summed = jnp.where(lane < TILE, summed, 1.0)
    total = as_column(highest + jnp.log(summed))
    logprobs = shares[...] - total
    streams = out.shape[0]
    for b in range(streams):
        out[b, 0:1, :] = logprobs[b : b + 1, :]
        out[b, 1:2, :] = logprobs[streams + b : streams + b + 1, :]


def body(
    token_ids,
    cache_lengths,
    embed_table,
    attn_gain,
    final_gain,
    w_qkv,
    w_out,
    cache_keys,
    cache_values,
):
    streams = token_ids.shape[1]
    rows = 2 * streams
    vocab_rows, local_width = embed_table.shape
    model_width = attn_gain.shape[0]
    seqs, peers = lax.axis_size(SEQ), lax.axis_size(TENSOR)
    tensor_index = lax.axis_index(TENSOR)
    slots_at = [slot_of(block) for block in range(peers)]
    place = lax.axis_index(SEQ).astype(jnp.int32).reshape(1)
    params = pltpu.CompilerParams(vmem_limit_bytes=16 * 1024 * 1024)
    shape = jax.ShapeDtypeStruct

    picked = pl.pallas_call(
        pick_kernel,
        out_shape=shape((seqs, TILE, HD), bf16),
        in_specs=[SMEM, SMEM, HBM],
        out_specs=VMEM,
        scratch_shapes=[
            pltpu.VMEM((rows, TILE, HD), bf16),
            pltpu.SemaphoreType.DMA((rows,)),
        ],
        compiler_params=pltpu.CompilerParams(vmem_limit_bytes=PICK_GRANT),
        cost_estimate=pl.CostEstimate(flops=0, bytes_accessed=2**17, transcendentals=0),
        name="pick",
    )(place, token_ids, embed_table)
    embedded = jnp.sum(exchange(picked, SEQ).astype(f32), 0).astype(bf16)
    gathered = exchange(jnp.broadcast_to(embedded, (peers, TILE, HD)), TENSOR[::-1])

    positions = (cache_lengths[None, :] + jnp.arange(2, dtype=jnp.int32)[:, None]).reshape(rows)
    half = HD // 2
    frequency = 10000.0 ** (-(jnp.arange(half, dtype=f32) * 2.0 / HD))
    angles = positions.astype(f32)[:, None] * frequency
    cosine, sine = jnp.cos(angles), jnp.sin(angles)
    padding = ((0, TILE - rows), (0, 0))
    cosine = jnp.pad(jnp.concatenate([cosine, cosine], 1), padding)
    sine = jnp.pad(jnp.concatenate([-sine, sine], 1), padding)

    w_qkv = jnp.moveaxis(w_qkv, 1, 0)
    w_rows = model_width * W_STAGED // 32
    parts, new_kv = pl.pallas_call(
        functools.partial(attend_kernel, slots_at),
        out_shape=(shape((seqs, TILE, HD), f32), shape((2, TILE, HD), bf16)),
        in_specs=[SMEM, SMEM] + [VMEM] * 5 + [HBM] * 3,
        out_specs=(VMEM, VMEM),
        scratch_shapes=[
            pltpu.VMEM((3, model_width - w_rows, HD), bf16),
            pltpu.VMEM(cache_keys.shape, bf16),
            pltpu.VMEM(cache_values.shape, bf16),
            pltpu.SemaphoreType.DMA((3,)),
        ],
        compiler_params=pltpu.CompilerParams(vmem_limit_bytes=ATTEND_GRANT),
        name="attend",
    )(
        place,
        cache_lengths,
        gathered,
        attn_gain.reshape(peers, HD),
        cosine,
        sine,
        staged(embedded, w_qkv, w_rows),
        w_qkv,
        cache_keys,
        cache_values,
    )
    mixed = pl.pallas_call(
        functools.partial(merge_kernel, rows, slots_at),
        out_shape=shape((peers, TILE, HD), bf16),
        in_specs=[VMEM, VMEM],
        out_specs=VMEM,
        compiler_params=params,
        name="merge",
    )(exchange(parts, SEQ), w_out)
    share_width = vocab_rows // peers
    staged_rows = STAGED * peers // 32 * share_width
    table_start = staged(mixed, embed_table, staged_rows)
    hidden, sent = pl.pallas_call(
        functools.partial(head_kernel, slots_at),
        out_shape=(shape((TILE, HD), bf16), shape((peers, TILE, share_width), bf16)),
        in_specs=[VMEM] * 4 + [HBM],
        out_specs=(VMEM, VMEM),
        scratch_shapes=[
            pltpu.VMEM((vocab_rows - staged_rows, HD), bf16),
            pltpu.SemaphoreType.DMA,
        ],
        compiler_params=pltpu.CompilerParams(vmem_limit_bytes=HEAD_GRANT),
        name="head",
    )(
        exchange(mixed, TENSOR[::-1]),
        embedded,
        lax.dynamic_slice_in_dim(final_gain, tensor_index * HD, HD).reshape(1, HD),
        table_start,
        embed_table,
    )
    everyone = seqs * peers
    shares, lines = pl.pallas_call(
        functools.partial(share_kernel, model_width),
        out_shape=(shape((TILE, share_width), f32), shape((everyone // 8, 8, HD), f32)),
        in_specs=[VMEM],
        out_specs=(VMEM, VMEM),
        compiler_params=params,
        name="share",
    )(exchange(sent, TENSOR[::-1]))
    logprobs = pl.pallas_call(
        finish_kernel,
        out_shape=shape((streams, 2, share_width), f32),
        in_specs=[VMEM, VMEM],
        out_specs=VMEM,
        compiler_params=params,
        name="finish",
    )(shares, exchange(lines.reshape(everyone, 1, HD), EVERYONE).reshape(lines.shape))
    return (
        hidden[:rows].reshape(2, streams, local_width),
        new_kv[:, :rows].reshape(2, 2, streams, local_width),
        jnp.swapaxes(logprobs, 0, 1),
    )


def solution(mesh):
    split = Mesh(mesh.devices.reshape(4, 2, 4, 8), ("seq_0", "seq_1", "tensor_0", "tensor_1"))
    placed = (
        P(),
        P(),
        P(SEQ, TENSOR),
        P(),
        P(),
        P(None, None, TENSOR),
        P(TENSOR, None),
        P(None, SEQ, TENSOR),
        P(None, SEQ, TENSOR),
    )
    return jax.shard_map(
        body,
        mesh=split,
        in_specs=placed,
        out_specs=(P(None, None, TENSOR), P(None, None, None, TENSOR), P(None, None, SEQ_TENSOR)),
        check_vma=False,
    )
```

```python
import functools
import math

import jax
import jax.numpy as jnp
from jax import lax
from jax.experimental import pallas as pl
from jax.experimental.pallas import tpu as pltpu
from jax.sharding import Mesh
from jax.sharding import PartitionSpec as P

HD = 128
TILE = 16
SEQ = ("seq_0", "seq_1")
TENSOR = ("tensor_0", "tensor_1")
SEQ_TENSOR = ("seq_0", "seq_1", "tensor_0", "tensor_1")
EVERYONE = ("tensor_1", "tensor_0", "seq_0", "seq_1")

epsilon = 1e-05
logit_gain = 2.0
lowest = -1e30
f32, bf16 = jnp.float32, jnp.bfloat16
VMEM = pl.BlockSpec(memory_space=pltpu.VMEM)
MIB = 1024 * 1024
PICK_GRANT = 61 * MIB
STAGE_GRANT = 49 * MIB + MIB // 2
ATTEND_GRANT = 203 * MIB // 4
HEAD_GRANT = 201 * MIB // 4
W_STAGED = 22
STAGED = 23
SMEM = pl.BlockSpec(memory_space=pltpu.SMEM)
HBM = pl.BlockSpec(memory_space=pltpu.HBM)


def slot_of(block):
    planes, depth = lax.axis_size(TENSOR[0]), lax.axis_size(TENSOR[1])
    return block % depth * planes + block // depth


def exchange(copies, axis):
    return lax.all_to_all(copies, axis, split_axis=0, concat_axis=0, tiled=True)


def row_of(width=HD):
    return lax.broadcasted_iota(jnp.int32, (TILE, width), 0)


def lane_of(width=HD):
    return lax.broadcasted_iota(jnp.int32, (TILE, width), 1)


def as_line(column):
    return jnp.sum(jnp.where(row_of() == lane_of(), column, 0.0), 0, keepdims=True)


def as_column(line):
    return jnp.sum(jnp.where(row_of() == lane_of(), line, 0.0), 1, keepdims=True)


def pick_kernel(place, ids, table, out, groups, sems):
    streams = ids.shape[1]
    vocab_rows = table.shape[0]
    within, copies = [], []
    for row in range(2 * streams):
        local = ids[row // streams, row % streams] - place[0] * vocab_rows
        inside = (local >= 0) & (local < vocab_rows)
        local = jnp.clip(local, 0, vocab_rows - 1)
        offset = lax.rem(local, TILE)
        start = pl.multiple_of(local - offset, TILE)
        copy = pltpu.make_async_copy(table.at[pl.ds(start, TILE)], groups.at[row], sems.at[row])
        copy.start()
        copies.append(copy)
        within.append(jnp.where(inside, offset, TILE))
    for copy in copies:
        copy.wait()
    total = jnp.zeros((TILE, HD), f32)
    for row in range(2 * streams):
        block = groups[row].astype(f32)
        found = jnp.sum(jnp.where(row_of() == within[row], block, 0.0), 0, keepdims=True)
        total = jnp.where(row_of() == row, found, total)
    picked = total.astype(bf16)
    for peer in range(out.shape[0]):
        out[peer] = picked


def stage_kernel(after, source, out, sems):
    del after
    lead = (slice(None),) * (len(source.shape) - 2)
    chunks = sems.shape[0]
    tall = out.shape[-2] // chunks
    copies = []
    for k in range(chunks):
        part = (*lead, pl.ds(k * tall, tall))
        copies.append(pltpu.make_async_copy(source.at[part], out.at[part], sems.at[k]))
        copies[-1].start()
    for copy in copies:
        copy.wait()


def staged(after, source, rows):
    shape = (*source.shape[:-2], rows, source.shape[-1])
    return pl.pallas_call(
        stage_kernel,
        out_shape=jax.ShapeDtypeStruct(shape, source.dtype),
        in_specs=[HBM, HBM],
        out_specs=VMEM,
        scratch_shapes=[pltpu.SemaphoreType.DMA((4,))],
        compiler_params=pltpu.CompilerParams(vmem_limit_bytes=STAGE_GRANT),
        cost_estimate=pl.CostEstimate(
            flops=0, bytes_accessed=4 * math.prod(shape), transcendentals=0
        ),
        name="stage",
    )(after, source)


def attend_kernel(
    slots_at,
    place,
    lengths,
    gathered,
    gain,
    cosine,
    sine,
    w_start,
    all_w_qkv,
    all_keys,
    all_values,
    out,
    new_kv,
    w_rest,
    keys,
    values,
    sems,
):
    streams, slots, _ = keys.shape
    first = w_start.shape[1]
    weight_copy = pltpu.make_async_copy(
        all_w_qkv.at[:, pl.ds(first, w_rest.shape[1])], w_rest, sems.at[0]
    )
    key_copy = pltpu.make_async_copy(all_keys, keys, sems.at[1])
    value_copy = pltpu.make_async_copy(all_values, values, sems.at[2])
    for copy in (weight_copy, key_copy, value_copy):
        copy.start()
    blocks = gathered.shape[0]
    width = blocks * HD
    seq = place[0]
    squares = jnp.zeros((TILE, HD), f32)
    for k in range(blocks):
        part = gathered[k].astype(f32)
        squares = squares + part * part
    scale = lax.rsqrt(jnp.sum(squares, 1, keepdims=True) / width + epsilon)
    normed = [
        (gathered[slots_at[k]].astype(f32) * scale * gain[k : k + 1]).astype(bf16) for k in range(blocks)
    ]
    begin = jnp.concatenate(normed[: first // HD], 1)
    rest = jnp.concatenate(normed[first // HD :], 1)
    query, key, value = (
        jnp.dot(begin, w_start[c], preferred_element_type=f32) for c in range(3)
    )
    weight_copy.wait()
    query, key, value = (
        total + jnp.dot(rest, w_rest[c], preferred_element_type=f32)
        for c, total in enumerate((query, key, value))
    )

    def rotated(part):
        return (part * cosine[...] + pltpu.roll(part, HD // 2, 1) * sine[...]).astype(bf16)

    query, key, value = rotated(query), rotated(key), value.astype(bf16)
    new_kv[0] = key
    new_kv[1] = value

    inverse = HD ** (-0.5)
    over_lanes = (((1,), (1,)), ((), ()))
    rows = row_of(slots)
    scores = jnp.zeros((TILE, slots), f32)
    length = jnp.zeros((TILE, 1), jnp.int32)
    first_lane = row_of(1)
    key_copy.wait()
    for b in range(streams):
        mine = (rows == b) | (rows == streams + b)
        some = lax.dot_general(query, keys[b], over_lanes, preferred_element_type=f32)
        scores = jnp.where(mine, some, scores)
        length = jnp.where(
            (first_lane == b) | (first_lane == streams + b), lengths[b], length
        )
    visible = lane_of(slots) + seq * slots < length
    scores = jnp.where(visible, scores * inverse, lowest)

    row, lane = row_of(TILE), lane_of(TILE)
    step, lane_step = (row >= streams).astype(jnp.int32), (lane >= streams).astype(jnp.int32)
    allowed = (row - step * streams == lane - lane_step * streams) & (lane_step <= step)
    allowed = allowed & (row < 2 * streams) & (lane < 2 * streams) & (seq == 0)
    fresh = lax.dot_general(query, key, over_lanes, preferred_element_type=f32)
    fresh = jnp.where(allowed, fresh * inverse, lowest)

    highest = jnp.maximum(jnp.max(scores, 1, keepdims=True), jnp.max(fresh, 1, keepdims=True))
    weights = jnp.where(visible, jnp.exp(scores - highest), 0.0)
    fresh_weights = jnp.where(allowed, jnp.exp(fresh - highest), 0.0)
    total = jnp.sum(weights, 1, keepdims=True) + jnp.sum(fresh_weights, 1, keepdims=True)
    mixed = jnp.dot(fresh_weights.astype(bf16), value, preferred_element_type=f32)
    value_copy.wait()
    for b in range(streams):
        mine = (rows == b) | (rows == streams + b)
        share = jnp.where(mine, weights, 0.0).astype(bf16)
        mixed = mixed + jnp.dot(share, values[b], preferred_element_type=f32)
    sent = jnp.where(row_of() == TILE - 2, as_line(highest), mixed)
    sent = jnp.where(row_of() == TILE - 1, as_line(total), sent)
    for peer in range(out.shape[0]):
        out[peer] = sent


def merge_kernel(rows, slots_at, parts, w_out, out):
    count = parts.shape[0]
    peaks = jnp.concatenate([parts[k, TILE - 2 : TILE - 1, :] for k in range(count)], 0)
    sums = jnp.concatenate([parts[k, TILE - 1 : TILE, :] for k in range(count)], 0)
    scales = jnp.exp(peaks - jnp.max(peaks, 0, keepdims=True))
    denominator = as_column(jnp.sum(sums * scales, 0, keepdims=True))
    numerator = jnp.zeros((TILE, HD), f32)
    for k in range(count):
        numerator = numerator + parts[k] * as_column(scales[k : k + 1, :])
    real = row_of() < rows
    attended = jnp.where(real, numerator / jnp.where(real, denominator, 1.0), 0.0).astype(bf16)
    per = 8
    for group in range(out.shape[0] // per):
        some = jnp.dot(
            attended, w_out[:, group * per * HD : (group + 1) * per * HD], preferred_element_type=f32
        ).astype(bf16)
        for k in range(per):
            out[slots_at[group * per + k]] = some[:, k * HD : (k + 1) * HD]


def head_kernel(slots_at, parts, embedded, gain, staged, whole_table, hidden_out, out, table, sem):
    peers, _, share = out.shape
    first = staged.shape[0] // share
    rest = pltpu.make_async_copy(
        whole_table.at[pl.ds(first * share, table.shape[0])], table, sem
    )
    rest.start()
    mixed = jnp.zeros((TILE, HD), f32)
    for k in range(parts.shape[0]):
        mixed = mixed + parts[k].astype(f32)
    hidden = (embedded[...].astype(f32) + mixed).astype(bf16)
    hidden_out[...] = hidden
    wide = hidden.astype(f32)
    squares = as_line(jnp.sum(wide * wide, 1, keepdims=True))
    high = squares.astype(bf16).astype(f32)
    middle = (squares - high).astype(bf16).astype(f32)
    low = squares - high - middle
    line = jnp.concatenate([high, middle, low, jnp.zeros((1, share - 3 * HD), f32)], 1)
    gated = (wide * gain[...]).astype(bf16)
    spare = row_of(share) == TILE - 1
    for k in range(peers):
        source, at = (staged, k) if k < first else (table, k - first)
        if k == first:
            rest.wait()
        some = lax.dot_general(
            gated,
            source[at * share : (at + 1) * share, :],
            (((1,), (1,)), ((), ())),
            preferred_element_type=f32,
        )
        out[slots_at[k]] = jnp.where(spare, line, some).astype(bf16)


def share_kernel(model_width, parts, shares_out, lines_out):
    total = parts[0].astype(f32)
    for k in range(1, parts.shape[0]):
        total = total + parts[k].astype(f32)
    line = total[TILE - 1 :, :]
    squares = as_column(line[:, :HD] + line[:, HD : 2 * HD] + line[:, 2 * HD : 3 * HD])
    factor = lax.rsqrt(squares / model_width + epsilon) * (logit_gain / math.sqrt(model_width))
    shares = total * factor
    shares_out[...] = shares
    highest = jnp.max(shares, 1, keepdims=True)
    summed = jnp.sum(jnp.exp(shares - highest), 1, keepdims=True)
    sent = as_line(highest) + pltpu.roll(as_line(summed), HD // 2, 1)
    lines_out[...] = jnp.broadcast_to(sent.reshape(1, 1, HD), lines_out.shape)


def finish_kernel(shares, lines, out):
    every = lines[...]
    highest = jnp.max(jnp.max(every, 0), 0, keepdims=True)
    scaled = jnp.exp(every - highest.reshape(1, 1, HD)) * pltpu.roll(every, HD // 2, 2)
    summed = jnp.sum(jnp.sum(scaled, 0), 0, keepdims=True)
    lane = lax.broadcasted_iota(jnp.int32, summed.shape, 1)
    summed = jnp.where(lane < TILE, summed, 1.0)
    total = as_column(highest + jnp.log(summed))
    logprobs = shares[...] - total
    streams = out.shape[0]
    for b in range(streams):
        out[b, 0:1, :] = logprobs[b : b + 1, :]
        out[b, 1:2, :] = logprobs[streams + b : streams + b + 1, :]


def body(
    token_ids,
    cache_lengths,
    embed_table,
    attn_gain,
    final_gain,
    w_qkv,
    w_out,
    cache_keys,
    cache_values,
):
    streams = token_ids.shape[1]
    rows = 2 * streams
    vocab_rows, local_width = embed_table.shape
    model_width = attn_gain.shape[0]
    seqs, peers = lax.axis_size(SEQ), lax.axis_size(TENSOR)
    tensor_index = lax.axis_index(TENSOR)
    slots_at = [slot_of(block) for block in range(peers)]
    place = lax.axis_index(SEQ).astype(jnp.int32).reshape(1)
    params = pltpu.CompilerParams(vmem_limit_bytes=16 * 1024 * 1024)
    shape = jax.ShapeDtypeStruct

    picked = pl.pallas_call(
        pick_kernel,
        out_shape=shape((seqs, TILE, HD), bf16),
        in_specs=[SMEM, SMEM, HBM],
        out_specs=VMEM,
        scratch_shapes=[
            pltpu.VMEM((rows, TILE, HD), bf16),
            pltpu.SemaphoreType.DMA((rows,)),
        ],
        compiler_params=pltpu.CompilerParams(vmem_limit_bytes=PICK_GRANT),
        cost_estimate=pl.CostEstimate(flops=0, bytes_accessed=2**17, transcendentals=0),
        name="pick",
    )(place, token_ids, embed_table)
    embedded = jnp.sum(exchange(picked, SEQ).astype(f32), 0).astype(bf16)
    gathered = exchange(jnp.broadcast_to(embedded, (peers, TILE, HD)), TENSOR[::-1])

    positions = (cache_lengths[None, :] + jnp.arange(2, dtype=jnp.int32)[:, None]).reshape(rows)
    half = HD // 2
    frequency = 10000.0 ** (-(jnp.arange(half, dtype=f32) * 2.0 / HD))
    angles = positions.astype(f32)[:, None] * frequency
    cosine, sine = jnp.cos(angles), jnp.sin(angles)
    padding = ((0, TILE - rows), (0, 0))
    cosine = jnp.pad(jnp.concatenate([cosine, cosine], 1), padding)
    sine = jnp.pad(jnp.concatenate([-sine, sine], 1), padding)

    w_qkv = jnp.moveaxis(w_qkv, 1, 0)
    w_rows = model_width * W_STAGED // 32
    parts, new_kv = pl.pallas_call(
        functools.partial(attend_kernel, slots_at),
        out_shape=(shape((seqs, TILE, HD), f32), shape((2, TILE, HD), bf16)),
        in_specs=[SMEM, SMEM] + [VMEM] * 5 + [HBM] * 3,
        out_specs=(VMEM, VMEM),
        scratch_shapes=[
            pltpu.VMEM((3, model_width - w_rows, HD), bf16),
            pltpu.VMEM(cache_keys.shape, bf16),
            pltpu.VMEM(cache_values.shape, bf16),
            pltpu.SemaphoreType.DMA((3,)),
        ],
        compiler_params=pltpu.CompilerParams(vmem_limit_bytes=ATTEND_GRANT),
        name="attend",
    )(
        place,
        cache_lengths,
        gathered,
        attn_gain.reshape(peers, HD),
        cosine,
        sine,
        staged(embedded, w_qkv, w_rows),
        w_qkv,
        cache_keys,
        cache_values,
    )
    mixed = pl.pallas_call(
        functools.partial(merge_kernel, rows, slots_at),
        out_shape=shape((peers, TILE, HD), bf16),
        in_specs=[VMEM, VMEM],
        out_specs=VMEM,
        compiler_params=params,
        name="merge",
    )(exchange(parts, SEQ), w_out)
    share_width = vocab_rows // peers
    staged_rows = STAGED * peers // 32 * share_width
    table_start = staged(mixed, embed_table, staged_rows)
    hidden, sent = pl.pallas_call(
        functools.partial(head_kernel, slots_at),
        out_shape=(shape((TILE, HD), bf16), shape((peers, TILE, share_width), bf16)),
        in_specs=[VMEM] * 4 + [HBM],
        out_specs=(VMEM, VMEM),
        scratch_shapes=[
            pltpu.VMEM((vocab_rows - staged_rows, HD), bf16),
            pltpu.SemaphoreType.DMA,
        ],
        compiler_params=pltpu.CompilerParams(vmem_limit_bytes=HEAD_GRANT),
        name="head",
    )(
        exchange(mixed, TENSOR[::-1]),
        embedded,
        lax.dynamic_slice_in_dim(final_gain, tensor_index * HD, HD).reshape(1, HD),
        table_start,
        embed_table,
    )
    everyone = seqs * peers
    shares, lines = pl.pallas_call(
        functools.partial(share_kernel, model_width),
        out_shape=(shape((TILE, share_width), f32), shape((everyone // 8, 8, HD), f32)),
        in_specs=[VMEM],
        out_specs=(VMEM, VMEM),
        compiler_params=params,
        name="share",
    )(exchange(sent, TENSOR[::-1]))
    logprobs = pl.pallas_call(
        finish_kernel,
        out_shape=shape((streams, 2, share_width), f32),
        in_specs=[VMEM, VMEM],
        out_specs=VMEM,
        compiler_params=params,
        name="finish",
    )(shares, exchange(lines.reshape(everyone, 1, HD), EVERYONE).reshape(lines.shape))
    return (
        hidden[:rows].reshape(2, streams, local_width),
        new_kv[:, :rows].reshape(2, 2, streams, local_width),
        jnp.swapaxes(logprobs, 0, 1),
    )


def solution(mesh):
    split = Mesh(mesh.devices.reshape(4, 2, 4, 8), ("seq_0", "seq_1", "tensor_0", "tensor_1"))
    placed = (
        P(),
        P(),
        P(SEQ, TENSOR),
        P(),
        P(),
        P(None, None, TENSOR),
        P(TENSOR, None),
        P(None, SEQ, TENSOR),
        P(None, SEQ, TENSOR),
    )
    return jax.shard_map(
        body,
        mesh=split,
        in_specs=placed,
        out_specs=(P(None, None, TENSOR), P(None, None, None, TENSOR), P(None, None, SEQ_TENSOR)),
        check_vma=False,
    )
```
